512 devices in a mesh: dp: 16 (over z_lo, core), ctx: 32 (over y, x, z_hi).
Axes of the slice: x: 4, y: 4, z: 16 (z_hi: 2, z_lo: 8; z = z_hi * 8 + z_lo), core: 2. Of those that a mesh axis runs over, the one named last changes fastest.
Arguments:
- normed: bfloat16 [65536, 8192], P(('dp', 'ctx')), may hold values from -24 to 24
- query: bfloat16 [65536, 512], P(('dp', 'ctx')), may hold values from -162 to 162
- key_value: bfloat16 [65536, 256], P(('dp', 'ctx')), may hold values from -6 to 6
- output_grad: bfloat16 [65536, 512], P(('dp', 'ctx')), may hold values from -6 to 6
- lengths: int32 [16, 16], P('dp'), may hold values from 1 to 1024, 4096 in all within a row
- advantage: float32 [16, 16], P('dp'), may hold values from -4 to 4
- span_plan: int32 [16, 32, 32], P('dp'), may hold values from 0 to 31, each once within a row
Outputs:
- query_grad: bfloat16 [65536, 512], P(('dp', 'ctx'))
- key_value_grad: bfloat16 [65536, 256], P(('dp', 'ctx'))
- weight_grad: bfloat16 [8192, 256], P(('ctx', 'dp'))
The draws below stay inside these ranges and needn't reach their ends.
Inputs may be any that keep to these rules, and one draw needn't show every extreme that they name: Each row holds the lengths of the 16 documents of one group in order; they sum to 4096 and the longest is exactly 1024. span_plan[g, s, c] is the block of 4 rows, counted within the rows of device s of group g, that span c takes; for each g and s the entries over c are a permutation.
All inputs are finite; a program needn't handle non-finite values.
Results may differ from the reference program's by a relative error of at most 0.029.
Values may be sent and summed in bfloat16 or wider, within the bound.
A program may use at most 64 MiB of HBM per device.

```python
import math
import jax
import jax.numpy as jnp
import numpy as np
from jax import lax

D = 8192
HD = 128
HQ = 4
TOK_DEV = 128
DOCS = 16
CONTEXT = 4096
LONGEST = 1024
TOKENS = 65536
N_DP = 16
N_CTX = 32


def shared_keys(key):
    base = jnp.clip(jax.random.normal(jax.random.fold_in(key, 50), (TOKENS, HD), jnp.float32), -6.0, 6.0)
    return base


def draw_key_value(key, part):
    base = shared_keys(key)
    key = jax.random.fold_in(key, 3)
    values = jnp.clip(jax.random.normal(key, (TOKENS, HD), jnp.float32), -6.0, 6.0)
    keys = base
    return jnp.concatenate([keys, values], axis=1).astype(jnp.bfloat16)


def draw_query(key, part):
    key = jax.random.fold_in(key, 4)
    drawn = jnp.clip(jax.random.normal(key, (TOKENS, HQ * HD), jnp.float32), -6.0, 6.0)
    return drawn.astype(jnp.bfloat16)


def with_spikes(values, rng, source, target, blocks, factor):
    def block_of(axis_at):
        return (jnp.arange(values.shape[axis_at]) // (values.shape[axis_at] // blocks)).reshape((-1,) + (1,) * (values.ndim - 1 - axis_at))

    near = jax.random.permutation(rng, blocks)[block_of(target)]
    far = (block_of(target) + blocks // 2) % blocks
    return jnp.where((block_of(source) == near) | (block_of(source) == far), factor * values, values)


def block_scale(own_key, extent, pieces, smallest, high):
    def one(axis_at, shards_of):
        draws = jax.random.uniform(jax.random.fold_in(jax.random.fold_in(own_key, 6), axis_at), (shards_of,), jnp.float32, smallest / len(pieces), high / len(pieces))
        return jnp.repeat(jnp.exp(draws), extent[axis_at] // shards_of).reshape((-1,) + (1,) * (len(extent) - axis_at - 1))

    gain = one(*pieces[0])
    for cut in pieces[1:]:
        gain = gain * one(*cut)
    return gain


def split_up(count, total, bound, slope):
    loads = [(1 << 20) // math.isqrt(standing ** slope) + 1 for standing in range(2, count + 1)]
    spare, counts = total - bound - (count - 1), [1] * (count - 1)
    while spare > 0:
        candidates = [i for i in range(count - 1) if counts[i] < bound]
        whole, budget = sum([loads[i] for i in candidates]), spare
        for i in candidates:
            extra = min(bound - counts[i], max(1, budget * loads[i] // whole), spare)
            counts[i] = counts[i] + extra
            spare = spare - extra
    return np.array([bound] + counts)


def uneven(own_key, count, total, reach, skew):
    if count == 2:
        one = jax.random.randint(own_key, (), max(1, total - reach), min(reach, total - 1) + 1)
        return jnp.stack([one, total - one])
    sizes = jnp.asarray(split_up(count, total, reach, skew), jnp.int32)
    couples = (count - 1) // 2
    donor, receiver = sizes[1:1 + 2 * couples:2], sizes[2:2 + 2 * couples:2]
    room = jnp.minimum(donor - 1, reach - receiver)
    passed = jax.random.randint(jax.random.fold_in(own_key, 1), (couples,), 0, 1 << 20) % (room + 1)
    sizes = sizes.at[1:1 + 2 * couples:2].set(donor - passed).at[2:2 + 2 * couples:2].set(receiver + passed)
    return sizes[jax.random.permutation(jax.random.fold_in(own_key, 2), count)]


def gaussian(rng, extent, spread, bound, pieces=(), held_as=jnp.bfloat16):
    entries = jax.random.normal(rng, extent, jnp.float32) * spread
    if len(pieces) > 0:
        entries = block_scale(rng, extent, pieces, -0.22, 0.18) * entries
    return jnp.clip(entries, min=-bound, max=bound).astype(held_as)


def heavy_noise(rng, extent, spread, most, shards, heavy, kind=jnp.bfloat16):
    entries = spread * jax.random.normal(rng, extent, jnp.float32)
    if shards:
        entries = entries * block_scale(rng, extent, shards, -0.22, 0.18)
    return jnp.clip(with_spikes(entries, jax.random.fold_in(rng, 3), *heavy), -most, most).astype(kind)


def setup_inputs(seed: int = 0) -> dict:
    key_list = jax.random.split(jax.random.key(seed), 8)
    normed = heavy_noise(key_list[0], (TOKENS, D), 1.0, 24.0, ((0, 512),), (0, 1, 512, 6.0))
    query = draw_query(jax.random.fold_in(key_list[7], 71), 0)
    key_value = draw_key_value(jax.random.fold_in(key_list[7], 71), 0)
    output_grad = gaussian(key_list[3], (TOKENS, HQ * HD), 1.0, 6.0, ((0, 512),))
    lengths = jax.vmap(lambda own: uneven(own, DOCS, CONTEXT, LONGEST, 2))(jax.random.split(key_list[4], N_DP)).reshape((N_DP, DOCS)).astype(jnp.int32)
    advantage = gaussian(key_list[5], (N_DP, DOCS), 1.0, 4.0, ((0, 16),), jnp.float32)
    span_plan = jax.vmap(lambda own: jax.random.permutation(own, N_CTX))(jax.random.split(key_list[6], N_DP * N_CTX)).reshape((N_DP, N_CTX, N_CTX)).astype(jnp.int32)
    return dict(normed=normed, query=query, key_value=key_value, output_grad=output_grad, lengths=lengths, advantage=advantage, span_plan=span_plan)


NEG_FILL = -1.0e30


def doc_index(lengths, positions):
    doc_ends = jnp.cumsum(lengths)
    return jnp.sum((positions[:, None] >= doc_ends[None, :]).astype(jnp.int32), axis=1)


def per_token(doc_table, token_docs):
    matches = token_docs[:, None] == jnp.arange(doc_table.shape[0], dtype=jnp.int32)[None, :]
    return jnp.sum(jnp.where(matches, doc_table[None, :], jnp.zeros((), doc_table.dtype)), axis=1)


def group_backward(normed, query, key_value, output_grad, lengths, advantage, span_plan):
    context = TOK_DEV * N_CTX
    rows_per_block = TOK_DEV // N_CTX
    score_scale = HD ** -0.5
    positions = jnp.arange(context, dtype=jnp.int32)
    token_docs = doc_index(lengths, positions)
    weighted = (per_token(advantage, token_docs)[:, None] * output_grad.astype(jnp.float32)).astype(jnp.bfloat16)
    keys = key_value[:, :HD].astype(jnp.float32)
    values = key_value[:, HD:].astype(jnp.float32)

    def one_span(totals, span):
        span_pos = (jnp.arange(N_CTX, dtype=jnp.int32)[:, None] * TOK_DEV
                     + span_plan[:, span].astype(jnp.int32)[:, None] * rows_per_block
                     + jnp.arange(rows_per_block, dtype=jnp.int32)[None, :]).reshape(TOK_DEV)
        span_docs = token_docs[span_pos]
        q_rows = query[span_pos].astype(jnp.float32).reshape(TOK_DEV, HQ, HD)
        o_rows = weighted[span_pos].astype(jnp.float32).reshape(TOK_DEV, HQ, HD)
        visible = (span_docs[:, None] == token_docs[None, :]) & (span_pos[:, None] >= positions[None, :])
        scores = jnp.einsum("qhe,ke->hqk", q_rows, keys) * score_scale
        scores = jnp.where(visible[None], scores, NEG_FILL)
        row_max = jnp.max(scores, axis=-1, keepdims=True)
        log_total = row_max + jnp.log(jnp.sum(jnp.exp(scores - row_max), axis=-1, keepdims=True))
        prob_full = jnp.exp(scores - log_total)
        grad_prob = jnp.einsum("qhe,ke->hqk", o_rows, values)
        row_dot = jnp.sum(prob_full * grad_prob, axis=-1, keepdims=True)
        grad_score = lax.optimization_barrier((prob_full * (grad_prob - row_dot)).astype(jnp.bfloat16)).astype(jnp.float32)
        prob_low = lax.optimization_barrier(prob_full.astype(jnp.bfloat16)).astype(jnp.float32)
        query_grad = (jnp.einsum("hqk,ke->qhe", grad_score, keys) * score_scale).reshape(TOK_DEV, HQ * HD).astype(jnp.bfloat16)
        key_grad = jnp.einsum("hqk,qhe->ke", grad_score, q_rows) * score_scale
        value_grad = jnp.einsum("hqk,qhe->ke", prob_low, o_rows)
        partial_low = lax.optimization_barrier(jnp.concatenate([key_grad, value_grad], axis=1).astype(jnp.bfloat16))
        return totals + partial_low.astype(jnp.float32), query_grad

    start_totals = jnp.zeros((context, 2 * HD), jnp.float32)
    totals, span_grads = lax.scan(one_span, start_totals, jnp.arange(N_CTX, dtype=jnp.int32))
    key_value_grad = totals.astype(jnp.bfloat16)
    weight_term = jnp.dot(normed.T, key_value_grad, preferred_element_type=jnp.float32)
    return span_grads.reshape(context, HQ * HD), key_value_grad, weight_term


def reference(normed, query, key_value, output_grad, lengths, advantage, span_plan):
    context = TOK_DEV * N_CTX
    grouped = (normed.reshape(N_DP, context, D), query.reshape(N_DP, context, HQ * HD),
               key_value.reshape(N_DP, context, 2 * HD), output_grad.reshape(N_DP, context, HQ * HD),
               lengths, advantage, span_plan)

    def per_group(items):
        return group_backward(*items)

    query_grad, key_value_grad, weight_terms = lax.map(per_group, grouped)
    weight_grad = (jnp.sum(weight_terms, axis=0) * (TOKENS ** -0.5)).astype(jnp.bfloat16)
    return (query_grad.reshape(TOKENS, HQ * HD), key_value_grad.reshape(TOKENS, 2 * HD), weight_grad)
```

```python
import jax
import jax.numpy as jnp
from jax import lax
from jax.experimental import pallas as pl
from jax.experimental.pallas import tpu as pltpu
from jax.sharding import PartitionSpec as P

NEG_FILL = -1e30
MESH = pl.DeviceIdType.MESH
T = 128
HQ = 4
HD = 128
SEEN = 5
FEAT = 512
SCALE = HD**-0.5
FIRST = 7


def dot_nt(a, b):
    return lax.dot_general(a, b, (((1,), (1,)), ((), ())), preferred_element_type=jnp.float32)


def dot_nn(a, b):
    return lax.dot_general(a, b, (((1,), (0,)), ((), ())), preferred_element_type=jnp.float32)


def kernel(normed, query, kv, og, lengths, advantage, plan, qg_out, kvg_out, wg_out,
           q_in, og_in, q_st, o_st, kvb, k_t, bias, p_st, ds_st, onehot, part, got, own_far, far_sum, far_got,
           q_send, q_recv, x_got, x_t, g_all, w_acc, w_pair, w_pair_got, w_z, w_z_got,
           loc_sem, kz_s, kz_r, kp_s, kp_r, kf_s, kf_r, x_s, x_r, d_s, d_r, dz_s, dz_r, qa_s, qa_r, g_s, g_r, pr_s, pr_r, z_s, z_r):
    d = lax.axis_index("dp")
    c = lax.axis_index("ctx")
    j, p = c // 2, c % 2
    z_lo, core = d // 2, d % 2
    z = p * 8 + z_lo

    def plane(offset):
        return (d, lax.rem(j + offset, 16) * 2 + p)

    partner = (d, j * 2 + (1 - p))
    twin = (z_lo * 2 + (1 - core), c)

    def along_z(offset):
        there = lax.rem(z + offset, 16)
        return (lax.rem(there, 8) * 2 + core, j * 2 + there // 8)

    def remote(src, dst, send, recv, where):
        return pltpu.make_async_remote_copy(src_ref=src, dst_ref=dst, send_sem=send, recv_sem=recv,
                                            device_id=where, device_id_type=MESH)

    loads = [
        pltpu.make_async_copy(query, q_in, loc_sem.at[0]),
        pltpu.make_async_copy(og, og_in, loc_sem.at[1]),
        pltpu.make_async_copy(kv, kvb.at[0], loc_sem.at[2]),
        pltpu.make_async_copy(normed.at[:, pl.ds(pl.multiple_of(j * FEAT, FEAT), FEAT)], x_got.at[j], loc_sem.at[3]),
    ]
    for cp in loads:
        cp.start()

    barrier = pltpu.get_barrier_semaphore()

    def greet_ctx(o, carry):
        pl.semaphore_signal(barrier, inc=1, device_id=(d, lax.rem(c + o, 32)), device_id_type=MESH)
        return carry

    def greet_z(o, carry):
        pl.semaphore_signal(barrier, inc=1, device_id=along_z(o), device_id_type=MESH)
        return carry

    lax.fori_loop(1, 32, greet_ctx, 0)
    lax.fori_loop(1, 8, greet_z, 0)
    lax.fori_loop(9, 16, greet_z, 0)
    pl.semaphore_signal(barrier, inc=1, device_id=twin, device_id_type=MESH)
    pl.semaphore_wait(barrier, 46)

    halves = [pl.ds(0, HD), pl.ds(HD, HD)]
    kz = [remote(kv.at[:, half], kvb.at[SEEN, :, half], kz_s.at[i], kz_r.at[i], partner) for i, half in enumerate(halves)]
    for cp in kz:
        cp.start()
    kp = [remote(kv, kvb.at[o], kp_s.at[o - 1], kp_r.at[o - 1], plane(o)) for o in range(1, SEEN)]
    for cp in kp:
        cp.start()

    def x_copy(o):
        there = lax.rem(j + o, 16)
        return remote(normed.at[:, pl.ds(pl.multiple_of(there * FEAT, FEAT), FEAT)], x_got.at[j],
                      x_s.at[o - 1], x_r.at[o - 1], plane(o))

    def x_start(o, carry):
        x_copy(o).start()
        return carry

    lax.fori_loop(1, FIRST + 1, x_start, 0)

    lanes = lax.broadcasted_iota(jnp.int32, (1, T), 1)
    rows = lax.broadcasted_iota(jnp.int32, (T, HD), 0)
    pos_lane = c * T + lanes
    pos_row = c * T + rows
    start_lane = jnp.zeros((1, T), jnp.int32)
    adv_row = jnp.zeros((T, HD), jnp.float32)
    end = jnp.int32(0)
    for i in range(16):
        begin = end
        end = end + lengths[0, i]
        start_lane = jnp.where(pos_lane >= begin, begin, start_lane)
        adv_row = jnp.where(pos_row >= begin, advantage[0, i], adv_row)
    key_rows = lax.broadcasted_iota(jnp.int32, (T, T), 0)
    for rel in range(2):
        for o in range(SEEN):
            key_plane = p if rel == 0 else 1 - p
            base = ((j - o) * 2 + key_plane) * T
            seen = (key_rows >= start_lane - base) & (key_rows <= pos_lane - base)
            bias[pl.ds((rel * SEEN + o) * T, T), :] = jnp.where(seen, 0.0, NEG_FILL)

    plan_row = plan[pl.ds(c, 1), :]
    out_row = lax.broadcasted_iota(jnp.int32, (4 * T, 32), 0)
    span_no = lax.broadcasted_iota(jnp.int32, (4 * T, 32), 1)
    block = jnp.sum(jnp.where(out_row // 16 == span_no, jnp.broadcast_to(plan_row, (4 * T, 32)), 0), axis=1, keepdims=True)
    row_no = lax.broadcasted_iota(jnp.int32, (4 * T, 1), 0)
    source = (row_no // 4 % 4) * T + block * 4 + row_no % 4
    for h in range(HQ):
        col_no = lax.broadcasted_iota(jnp.int32, (4 * T, T), 1) + h * T
        onehot[:, pl.ds(h * T, T)] = jnp.where(col_no == source, 1.0, 0.0).astype(jnp.bfloat16)

    loads[0].wait()
    loads[1].wait()
    for h in range(HQ):
        cols = pl.ds(h * HD, HD)
        q_st[pl.ds(h * T, T), :] = q_in[:, cols]
        o_st[pl.ds(h * T, T), :] = (adv_row * og_in[:, cols].astype(jnp.float32)).astype(jnp.bfloat16)

    kf = []
    for i, half in enumerate(halves):
        kz[i].wait_recv()
        for o in range(1, SEEN):
            cp = remote(kvb.at[SEEN, :, half], kvb.at[SEEN + o, :, half], kf_s.at[i * 4 + o - 1], kf_r.at[i * 4 + o - 1], plane(o))
            cp.start()
            kf.append(cp)
    loads[2].wait()
    for cp in kp:
        cp.wait_recv()
    for cp in kf:
        cp.wait_recv()

    n_keys = 2 * SEEN * T
    keys = kvb[:, :, :HD].reshape(n_keys, HD)
    values = kvb[:, :, HD:].reshape(n_keys, HD)
    for s in range(2 * SEEN):
        k_t[:, pl.ds(s * T, T)] = kvb[s, :, :HD].T
    for h in range(HQ):
        heads = pl.ds(h * T, T)
        scores = dot_nt(keys, q_st[heads, :]) * SCALE + bias[...]
        top = jnp.max(scores, axis=0, keepdims=True)
        weights = jnp.exp(scores - top)
        probs = weights * (1.0 / jnp.sum(weights, axis=0, keepdims=True))
        grad_prob = dot_nt(values, o_st[heads, :])
        row_dot = jnp.sum(probs * grad_prob, axis=0, keepdims=True)
        ds_st[:, heads] = (probs * (grad_prob - row_dot)).astype(jnp.bfloat16)
        p_st[:, heads] = probs.astype(jnp.bfloat16)

    half_rows = SEEN * T

    def grads(rel):
        at = pl.ds(rel * half_rows, half_rows)
        dk = dot_nn(ds_st[at, :], q_st[...]) * SCALE
        dv = dot_nn(p_st[at, :], o_st[...])
        return jnp.concatenate([dk, dv], axis=1)

    sent = []
    for rel in (1, 0):
        terms = grads(rel)
        own_far[rel] = terms[:T]
        part[pl.ds(rel * 4, 4)] = terms[T:].astype(jnp.bfloat16).reshape(SEEN - 1, T, 2 * HD)
        for o in range(1, SEEN):
            i = rel * 4 + o - 1
            cp = remote(part.at[i], got.at[i], d_s.at[i], d_r.at[i], plane(16 - o))
            cp.start()
            sent.append((rel, cp))

    q_grad_t = (dot_nn(k_t[...], ds_st[...]) * SCALE).astype(jnp.bfloat16)
    q_send[...] = dot_nt(onehot[...], q_grad_t).astype(jnp.bfloat16).reshape(32, 16, HD)
    q_recv[c] = q_send[c]

    def terms_sum(rel):
        for r, cp in sent:
            if r == rel:
                cp.wait_recv()
        total = own_far[rel]
        for o in range(SEEN - 1):
            total = total + got[rel * 4 + o].astype(jnp.float32)
        return total

    far_sum[...] = terms_sum(1).astype(jnp.bfloat16)
    dz = remote(far_sum, far_got, dz_s, dz_r, partner)
    dz.start()

    lax.fori_loop(FIRST + 1, 16, x_start, 0)

    def q_copy(o):
        there = lax.rem(c + o, 32)
        return remote(q_send.at[there], q_recv.at[c], qa_s.at[o - 1], qa_r.at[o - 1], (d, there))

    def q_start(o, carry):
        q_copy(o).start()
        return carry

    lax.fori_loop(1, 32, q_start, 0)

    near = terms_sum(0)

    loads[3].wait()

    def turn(b):
        x_t[:, pl.ds(pl.multiple_of(b * T, T), T)] = x_got[b].T

    turn(j)

    def x_take(o, carry):
        x_copy(o).wait_recv()
        turn(lax.rem(j + 16 - o, 16))
        return carry

    lax.fori_loop(1, FIRST + 1, x_take, 0)

    dz.wait_recv()
    kvg = (near + far_got[...].astype(jnp.float32)).astype(jnp.bfloat16)
    g_all[j] = kvg

    def g_copy(o):
        return remote(g_all.at[j], g_all.at[j], g_s.at[o - 1], g_r.at[o - 1], plane(o))

    def g_start(o, carry):
        g_copy(o).start()
        return carry

    lax.fori_loop(1, 16, g_start, 0)
    kvg_out[...] = kvg

    lax.fori_loop(FIRST + 1, 16, x_take, 0)

    def g_take(o, carry):
        g_copy(o).wait_recv()
        return carry

    lax.fori_loop(1, 16, g_take, 0)

    w_acc[...] = dot_nn(x_t[...], g_all[...].reshape(16 * T, 2 * HD)).reshape(16, 2, 16, 2 * HD)
    w_pair[...] = w_acc[:, 1 - core].astype(jnp.bfloat16)
    pair = remote(w_pair, w_pair_got, pr_s, pr_r, twin)
    pair.start()
    pair.wait_recv()
    w_z[...] = (w_acc[:, core] + w_pair_got[...].astype(jnp.float32)).astype(jnp.bfloat16)
    w_z_got[z] = w_z[z]

    def z_copy(o):
        return remote(w_z.at[lax.rem(z + o, 16)], w_z_got.at[z], z_s.at[o - 1], z_r.at[o - 1], along_z(o))

    def z_start(o, carry):
        z_copy(o).start()
        return carry

    lax.fori_loop(1, 16, z_start, 0)

    def q_take(o, carry):
        q_copy(o).wait_recv()
        return carry

    lax.fori_loop(1, 32, q_take, 0)
    arrived = q_recv[...].reshape(4 * T, HD)
    tok = lax.broadcasted_iota(jnp.int32, (T, 4 * T), 0)
    place = lax.broadcasted_iota(jnp.int32, (T, 4 * T), 1)
    for h in range(HQ):
        pick = jnp.where(place == tok // 4 * 16 + h * 4 + tok % 4, 1.0, 0.0).astype(jnp.bfloat16)
        qg_out[:, pl.ds(h * HD, HD)] = dot_nn(pick, arrived).astype(jnp.bfloat16)

    def z_take(o, carry):
        z_copy(o).wait_recv()
        return carry

    lax.fori_loop(1, 16, z_take, 0)
    total = jnp.sum(w_z_got[...].astype(jnp.float32), axis=0)
    wg_out[...] = (total * (1.0 / 256.0)).astype(jnp.bfloat16)

    for cp in kz + kp + kf + [cp for _, cp in sent] + [dz, pair]:
        cp.wait_send()

    def plane_sent(o, carry):
        x_copy(o).wait_send()
        g_copy(o).wait_send()
        z_copy(o).wait_send()
        return carry

    lax.fori_loop(1, 16, plane_sent, 0)

    def q_sent(o, carry):
        q_copy(o).wait_send()
        return carry

    lax.fori_loop(1, 32, q_sent, 0)


def local(normed, query, key_value, output_grad, lengths, advantage, span_plan):
    bf16, f32 = jnp.bfloat16, jnp.float32
    n_keys = 2 * SEEN * T
    dma = pltpu.SemaphoreType.DMA
    any_space = pl.BlockSpec(memory_space=pl.ANY)
    vmem = pl.BlockSpec(memory_space=pltpu.VMEM)
    smem = pl.BlockSpec(memory_space=pltpu.SMEM)
    return pl.pallas_call(
        kernel,
        out_shape=(
            jax.ShapeDtypeStruct((T, HQ * HD), bf16),
            jax.ShapeDtypeStruct((T, 2 * HD), bf16),
            jax.ShapeDtypeStruct((16, 2 * HD), bf16),
        ),
        in_specs=[any_space, any_space, any_space, any_space, smem, smem, vmem],
        out_specs=(vmem, vmem, vmem),
        scratch_shapes=[
            pltpu.VMEM((T, HQ * HD), bf16),
            pltpu.VMEM((T, HQ * HD), bf16),
            pltpu.VMEM((HQ * T, HD), bf16),
            pltpu.VMEM((HQ * T, HD), bf16),
            pltpu.VMEM((2 * SEEN, T, 2 * HD), bf16),
            pltpu.VMEM((HD, n_keys), bf16),
            pltpu.VMEM((n_keys, T), f32),
            pltpu.VMEM((n_keys, HQ * T), bf16),
            pltpu.VMEM((n_keys, HQ * T), bf16),
            pltpu.VMEM((HQ * T, HQ * T), bf16),
            pltpu.VMEM((8, T, 2 * HD), bf16),
            pltpu.VMEM((8, T, 2 * HD), bf16),
            pltpu.VMEM((2, T, 2 * HD), f32),
            pltpu.VMEM((T, 2 * HD), bf16),
            pltpu.VMEM((T, 2 * HD), bf16),
            pltpu.VMEM((32, 16, HD), bf16),
            pltpu.VMEM((32, 16, HD), bf16),
            pltpu.VMEM((16, T, FEAT), bf16),
            pltpu.VMEM((FEAT, 16 * T), bf16),
            pltpu.VMEM((16, T, 2 * HD), bf16),
            pltpu.VMEM((16, 2, 16, 2 * HD), f32),
            pltpu.VMEM((16, 16, 2 * HD), bf16),
            pltpu.VMEM((16, 16, 2 * HD), bf16),
            pltpu.VMEM((16, 16, 2 * HD), bf16),
            pltpu.VMEM((16, 16, 2 * HD), bf16),
            dma((4,)), dma((2,)), dma((2,)), dma((4,)), dma((4,)), dma((8,)), dma((8,)),
            dma((15,)), dma((15,)), dma((8,)), dma((8,)), dma, dma, dma((31,)), dma((31,)),
            dma((15,)), dma((15,)), dma, dma, dma((15,)), dma((15,)),
        ],
        compiler_params=pltpu.CompilerParams(collective_id=0, has_side_effects=True, vmem_limit_bytes=48 * 2**20),
        name="backward",
    )(normed, query, key_value, output_grad, lengths, advantage, span_plan.reshape(32, 32))


def solution(mesh):
    return jax.shard_map(
        local,
        mesh=mesh,
        in_specs=(
            P(("dp", "ctx"), None),
            P(("dp", "ctx"), None),
            P(("dp", "ctx"), None),
            P(("dp", "ctx"), None),
            P("dp", None),
            P("dp", None),
            P("dp", None, None),
        ),
        out_specs=(P(("dp", "ctx"), None), P(("dp", "ctx"), None), P(("ctx", "dp"), None)),
        check_vma=False,
    )
```

```python
import jax
import jax.numpy as jnp
from jax import lax
from jax.experimental import pallas as pl
from jax.experimental.pallas import tpu as pltpu
from jax.sharding import PartitionSpec as P

NEG_FILL = -1e30
MESH = pl.DeviceIdType.MESH
T = 128
HQ = 4
HD = 128
SEEN = 5
FEAT = 512
SCALE = HD**-0.5
OTHERS = [(0, 1), (1, 0), (1, 1), (2, 0), (2, 1), (3, 0), (3, 1)]


def dot_nt(a, b):
    return lax.dot_general(a, b, (((1,), (1,)), ((), ())), preferred_element_type=jnp.float32)


def dot_nn(a, b):
    return lax.dot_general(a, b, (((1,), (0,)), ((), ())), preferred_element_type=jnp.float32)


def kernel(normed, query, kv, og, lengths_in, advantage_in, plan_in, qg_out, kvg_out, wg_out,
           lengths, advantage, plan, q_in, og_in, q_st, o_st, kvb, k_t, bias, p_st, ds_st, onehot, part, got, own_far, far_sum, far_got,
           q_send, q_recv, x_in, x_t, x_all, g_all, w_acc, w_send, w_got, w_z, w_z_got,
           loc_sem, kz_s, kz_r, kp_s, kp_r, kf_s, kf_r, x_s, x_r, d_s, d_r, dz_s, dz_r, qa_s, qa_r, g_s, g_r, w_s, w_r, z_s, z_r):
    d = lax.axis_index("dp")
    c = lax.axis_index("ctx")
    j, p = c // 2, c % 2
    z_lo, core = d // 2, d % 2
    z = p * 8 + z_lo
    y, x = j // 4, lax.rem(j, 4)
    own_slot = (x * 2 + core, y * 2 + core)
    own_pos = (x, y)

    def plane(offset):
        return (d, lax.rem(j + offset, 16) * 2 + p)

    partner = (d, j * 2 + (1 - p))

    def line(axis, offset, flip):
        to_core = core if flip == 0 else 1 - core
        to_x = lax.rem(x + offset, 4) if axis == 0 else x
        to_y = lax.rem(y + offset, 4) if axis == 1 else y
        return (z_lo * 2 + to_core, (to_y * 4 + to_x) * 2 + p)

    def along_z(offset):
        there = lax.rem(z + offset, 16)
        return (lax.rem(there, 8) * 2 + core, j * 2 + there // 8)

    def remote(src, dst, send, recv, where):
        return pltpu.make_async_remote_copy(src_ref=src, dst_ref=dst, send_sem=send, recv_sem=recv,
                                            device_id=where, device_id_type=MESH)

    sends, recvs = [], []

    def launch(*cps):
        for cp in cps:
            cp.start()
            sends.append(cp)
            recvs.append(cp)

    def take(*cps):
        for cp in cps:
            recvs[:] = [r for r in recvs if r is not cp]
            cp.wait_recv()

    def launch_all(make, low, high):
        def step(o, carry):
            make(o).start()
            return carry

        lax.fori_loop(low, high, step, 0)
        sends.append((make, low, high))
        recvs.append((make, low, high))

    def take_all(make, low, high, then=None):
        def step(o, carry):
            make(o).wait_recv()
            if then is not None:
                then(o)
            return carry

        recvs[:] = [r for r in recvs if not (isinstance(r, tuple) and r[0] is make and r[1:] == (low, high))]
        lax.fori_loop(low, high, step, 0)

    loads = [
        pltpu.make_async_copy(query, q_in, loc_sem.at[0]),
        pltpu.make_async_copy(og, og_in, loc_sem.at[1]),
        pltpu.make_async_copy(kv, kvb.at[0], loc_sem.at[2]),
        pltpu.make_async_copy(normed, x_in, loc_sem.at[3]),
        pltpu.make_async_copy(lengths_in, lengths, loc_sem.at[4]),
        pltpu.make_async_copy(advantage_in, advantage, loc_sem.at[5]),
        pltpu.make_async_copy(plan_in.at[0], plan, loc_sem.at[6]),
    ]
    for cp in loads:
        cp.start()

    barrier = pltpu.get_barrier_semaphore()

    def greet_ctx(o, carry):
        pl.semaphore_signal(barrier, inc=1, device_id=(d, lax.rem(c + o, 32)), device_id_type=MESH)
        return carry

    def greet_z(o, carry):
        pl.semaphore_signal(barrier, inc=1, device_id=along_z(o), device_id_type=MESH)
        return carry

    lax.fori_loop(1, 32, greet_ctx, 0)
    lax.fori_loop(1, 8, greet_z, 0)
    lax.fori_loop(9, 16, greet_z, 0)
    for axis, offset in [(0, 0), (0, 1), (0, 2), (0, 3), (1, 1), (1, 2), (1, 3)]:
        pl.semaphore_signal(barrier, inc=1, device_id=line(axis, offset, 1), device_id_type=MESH)
    pl.semaphore_wait(barrier, 52)

    halves = [pl.ds(0, HD), pl.ds(HD, HD)]
    kz = [remote(kv.at[:, half], kvb.at[SEEN, :, half], kz_s.at[i], kz_r.at[i], partner) for i, half in enumerate(halves)]
    launch(*kz)
    kp = [remote(kv, kvb.at[o], kp_s.at[o - 1], kp_r.at[o - 1], plane(o)) for o in range(1, SEEN)]
    launch(*kp)

    loads[3].wait()

    def turn(at, carry):
        for q in range(4):
            block = x_in[:, pl.ds(pl.multiple_of(at * FEAT + q * T, T), T)].T
            for low in range(4):
                for k in range(2):
                    x_t[q // 2, k, at // 4, lax.rem(at, 4), pl.ds(((q % 2) * 4 + low) * 16, 16), :] = (
                        block[(low * 2 + k) * 16 : (low * 2 + k + 1) * 16])
        return carry

    lax.fori_loop(0, 16, turn, 0)

    def x_source(axis, offset, flip):
        to_core = core if flip == 0 else 1 - core
        if axis == 0:
            return x_t.at[0, to_core, :, lax.rem(x + offset, 4)]
        return x_t.at[1, to_core, lax.rem(y + offset, 4)]

    def x_place(axis):
        return x_all.at[axis, :, :, pl.ds(pl.multiple_of(own_slot[axis] * T, T), T)]

    x_copies = {}
    for axis in range(2):
        for offset, flip in OTHERS:
            m = axis * 7 + offset * 2 + flip - 1
            x_copies[axis, offset, flip] = remote(x_source(axis, offset, flip), x_place(axis), x_s.at[m], x_r.at[m], line(axis, offset, flip))
    x_own = [pltpu.make_async_copy(x_source(axis, 0, 0), x_place(axis), loc_sem.at[7 + axis]) for axis in range(2)]
    for cp in x_own:
        cp.start()
    launch(*[cp for (axis, offset, flip), cp in x_copies.items() if offset != 2])

    for cp in loads[4:]:
        cp.wait()
    lanes = lax.broadcasted_iota(jnp.int32, (1, T), 1)
    rows = lax.broadcasted_iota(jnp.int32, (T, HD), 0)
    pos_lane = c * T + lanes
    pos_row = c * T + rows
    start_lane = jnp.zeros((1, T), jnp.int32)
    adv_row = jnp.zeros((T, HD), jnp.float32)
    end = jnp.int32(0)
    for i in range(16):
        begin = end
        end = end + lengths[0, i]
        start_lane = jnp.where(pos_lane >= begin, begin, start_lane)
        adv_row = jnp.where(pos_row >= begin, advantage[0, i], adv_row)
    key_rows = lax.broadcasted_iota(jnp.int32, (T, T), 0)
    for rel in range(2):
        for o in range(SEEN):
            key_plane = p if rel == 0 else 1 - p
            base = ((j - o) * 2 + key_plane) * T
            seen = (key_rows >= start_lane - base) & (key_rows <= pos_lane - base)
            bias[pl.ds((rel * SEEN + o) * T, T), :] = jnp.where(seen, 0.0, NEG_FILL)

    plan_row = plan[pl.ds(c, 1), :]
    out_row = lax.broadcasted_iota(jnp.int32, (4 * T, 32), 0)
    span_no = lax.broadcasted_iota(jnp.int32, (4 * T, 32), 1)
    block = jnp.sum(jnp.where(out_row // 16 == span_no, jnp.broadcast_to(plan_row, (4 * T, 32)), 0), axis=1, keepdims=True)
    row_no = lax.broadcasted_iota(jnp.int32, (4 * T, 1), 0)
    source = (row_no // 4 % 4) * T + block * 4 + row_no % 4
    for h in range(HQ):
        col_no = lax.broadcasted_iota(jnp.int32, (4 * T, T), 1) + h * T
        onehot[:, pl.ds(h * T, T)] = jnp.where(col_no == source, 1.0, 0.0).astype(jnp.bfloat16)

    loads[0].wait()
    loads[1].wait()
    for h in range(HQ):
        cols = pl.ds(h * HD, HD)
        q_st[pl.ds(h * T, T), :] = q_in[:, cols]
        o_st[pl.ds(h * T, T), :] = (adv_row * og_in[:, cols].astype(jnp.float32)).astype(jnp.bfloat16)

    kf = []
    for i, half in enumerate(halves):
        take(kz[i])
        for o in range(1, SEEN):
            cp = remote(kvb.at[SEEN, :, half], kvb.at[SEEN + o, :, half], kf_s.at[i * 4 + o - 1], kf_r.at[i * 4 + o - 1], plane(o))
            launch(cp)
            kf.append(cp)
    loads[2].wait()
    take(*kp)
    take(*kf)

    n_keys = 2 * SEEN * T
    keys = kvb[:, :, :HD].reshape(n_keys, HD)
    values = kvb[:, :, HD:].reshape(n_keys, HD)
    for s in range(2 * SEEN):
        k_t[:, pl.ds(s * T, T)] = kvb[s, :, :HD].T
    for h in range(HQ):
        heads = pl.ds(h * T, T)
        scores = dot_nt(keys, q_st[heads, :]) * SCALE + bias[...]
        top = jnp.max(scores, axis=0, keepdims=True)
        weights = jnp.exp(scores - top)
        probs = weights * (1.0 / jnp.sum(weights, axis=0, keepdims=True))
        grad_prob = dot_nt(values, o_st[heads, :])
        row_dot = jnp.sum(probs * grad_prob, axis=0, keepdims=True)
        ds_st[:, heads] = (probs * (grad_prob - row_dot)).astype(jnp.bfloat16)
        p_st[:, heads] = probs.astype(jnp.bfloat16)

    half_rows = SEEN * T

    def grads(rel):
        at = pl.ds(rel * half_rows, half_rows)
        dk = dot_nn(ds_st[at, :], q_st[...]) * SCALE
        dv = dot_nn(p_st[at, :], o_st[...])
        return jnp.concatenate([dk, dv], axis=1)

    sent = []
    for rel in (1, 0):
        terms = grads(rel)
        own_far[rel] = terms[:T]
        part[pl.ds(rel * 4, 4)] = terms[T:].astype(jnp.bfloat16).reshape(SEEN - 1, T, 2 * HD)
        for o in range(1, SEEN):
            i = rel * 4 + o - 1
            cp = remote(part.at[i], got.at[i], d_s.at[i], d_r.at[i], plane(16 - o))
            launch(cp)
            sent.append((rel, cp))

    q_grad_t = (dot_nn(k_t[...], ds_st[...]) * SCALE).astype(jnp.bfloat16)
    q_send[...] = dot_nt(onehot[...], q_grad_t).astype(jnp.bfloat16).reshape(32, 16, HD)
    q_recv[c] = q_send[c]

    def terms_sum(rel):
        for r, cp in sent:
            if r == rel:
                take(cp)
        total = own_far[rel]
        for o in range(SEEN - 1):
            total = total + got[rel * 4 + o].astype(jnp.float32)
        return total

    far_sum[...] = terms_sum(1).astype(jnp.bfloat16)
    dz = remote(far_sum, far_got, dz_s, dz_r, partner)
    launch(dz)

    launch(*[cp for (axis, offset, flip), cp in x_copies.items() if offset == 2])

    near = terms_sum(0)

    take(dz)
    kvg = (near + far_got[...].astype(jnp.float32)).astype(jnp.bfloat16)
    g_copies = []
    for axis in range(2):
        g_all[axis, own_slot[axis]] = kvg
        for offset, flip in OTHERS:
            m = axis * 7 + offset * 2 + flip - 1
            slot = g_all.at[axis, own_slot[axis]]
            g_copies.append((axis, remote(slot, slot, g_s.at[m], g_r.at[m], line(axis, offset, flip))))
    launch(*[cp for _, cp in g_copies])
    kvg_out[...] = kvg

    def q_copy(o):
        there = lax.rem(c + o, 32)
        return remote(q_send.at[there], q_recv.at[c], qa_s.at[o - 1], qa_r.at[o - 1], (d, there))

    launch_all(q_copy, 1, 32)

    take(*x_copies.values())
    for cp in x_own:
        cp.wait()

    w_copies = []
    for axis in range(2):
        take(*[cp for a, cp in g_copies if a == axis])
        w_acc[axis] = dot_nn(x_all[axis].reshape(4 * T, 8 * T), g_all[axis].reshape(8 * T, 2 * HD)).reshape(4, T, 2 * HD)
        w_send[axis] = w_acc[axis].astype(jnp.bfloat16)
        for offset in range(1, 4):
            m = axis * 3 + offset - 1
            there = lax.rem(own_pos[1 - axis] + offset, 4)
            cp = remote(w_send.at[axis, there], w_got.at[m], w_s.at[m], w_r.at[m], line(1 - axis, offset, 0))
            launch(cp)
            w_copies.append((axis, cp))
    for axis in range(2):
        take(*[cp for a, cp in w_copies if a == axis])
        total = w_acc[axis, own_pos[1 - axis]]
        for offset in range(1, 4):
            total = total + w_got[axis * 3 + offset - 1].astype(jnp.float32)
        w_z[pl.ds(axis * 8, 8)] = total.astype(jnp.bfloat16).reshape(8, 16, 2 * HD)
    w_z_got[z] = w_z[z]

    def z_copy(o):
        return remote(w_z.at[lax.rem(z + o, 16)], w_z_got.at[z], z_s.at[o - 1], z_r.at[o - 1], along_z(o))

    launch_all(z_copy, 1, 16)

    take_all(q_copy, 1, 32)
    arrived = q_recv[...].reshape(4 * T, HD)
    tok = lax.broadcasted_iota(jnp.int32, (T, 4 * T), 0)
    place = lax.broadcasted_iota(jnp.int32, (T, 4 * T), 1)
    for h in range(HQ):
        pick = jnp.where(place == tok // 4 * 16 + h * 4 + tok % 4, 1.0, 0.0).astype(jnp.bfloat16)
        qg_out[:, pl.ds(h * HD, HD)] = dot_nn(pick, arrived).astype(jnp.bfloat16)

    take_all(z_copy, 1, 16)
    total = jnp.sum(w_z_got[...].astype(jnp.float32), axis=0)
    wg_out[...] = (total * (1.0 / 256.0)).astype(jnp.bfloat16)

    for item in sends:
        if isinstance(item, tuple):
            make, low, high = item

            def step(o, carry, make=make):
                make(o).wait_send()
                return carry

            lax.fori_loop(low, high, step, 0)
        else:
            item.wait_send()

def local(normed, query, key_value, output_grad, lengths, advantage, span_plan):
    bf16, f32 = jnp.bfloat16, jnp.float32
    n_keys = 2 * SEEN * T
    dma = pltpu.SemaphoreType.DMA
    vmem = pl.BlockSpec(memory_space=pltpu.VMEM)
    return pl.pallas_call(
        kernel,
        out_shape=(
            jax.ShapeDtypeStruct((T, HQ * HD), bf16),
            jax.ShapeDtypeStruct((T, 2 * HD), bf16),
            jax.ShapeDtypeStruct((16, 2 * HD), bf16),
        ),
        in_specs=[pl.BlockSpec(memory_space=pltpu.HBM)] * 7,
        out_specs=(vmem, vmem, vmem),
        scratch_shapes=[
            pltpu.SMEM((1, 16), jnp.int32),
            pltpu.SMEM((1, 16), f32),
            pltpu.VMEM((32, 32), jnp.int32),
            pltpu.VMEM((T, HQ * HD), bf16),
            pltpu.VMEM((T, HQ * HD), bf16),
            pltpu.VMEM((HQ * T, HD), bf16),
            pltpu.VMEM((HQ * T, HD), bf16),
            pltpu.VMEM((2 * SEEN, T, 2 * HD), bf16),
            pltpu.VMEM((HD, n_keys), bf16),
            pltpu.VMEM((n_keys, T), f32),
            pltpu.VMEM((n_keys, HQ * T), bf16),
            pltpu.VMEM((n_keys, HQ * T), bf16),
            pltpu.VMEM((HQ * T, HQ * T), bf16),
            pltpu.VMEM((8, T, 2 * HD), bf16),
            pltpu.VMEM((8, T, 2 * HD), bf16),
            pltpu.VMEM((2, T, 2 * HD), f32),
            pltpu.VMEM((T, 2 * HD), bf16),
            pltpu.VMEM((T, 2 * HD), bf16),
            pltpu.VMEM((32, 16, HD), bf16),
            pltpu.VMEM((32, 16, HD), bf16),
            pltpu.VMEM((T, 16 * FEAT), bf16),
            pltpu.VMEM((2, 2, 4, 4, T, T), bf16),
            pltpu.VMEM((2, 4, T, 8 * T), bf16),
            pltpu.VMEM((2, 8, T, 2 * HD), bf16),
            pltpu.VMEM((2, 4, T, 2 * HD), f32),
            pltpu.VMEM((2, 4, T, 2 * HD), bf16),
            pltpu.VMEM((6, T, 2 * HD), bf16),
            pltpu.VMEM((16, 16, 2 * HD), bf16),
            pltpu.VMEM((16, 16, 2 * HD), bf16),
            dma((9,)), dma((2,)), dma((2,)), dma((4,)), dma((4,)), dma((8,)), dma((8,)),
            dma((14,)), dma((14,)), dma((8,)), dma((8,)), dma, dma, dma((31,)), dma((31,)),
            dma((14,)), dma((14,)), dma((6,)), dma((6,)), dma((15,)), dma((15,)),
        ],
        compiler_params=pltpu.CompilerParams(collective_id=0, has_side_effects=True, vmem_limit_bytes=54 * 2**20),
        name="backward",
    )(normed, query, key_value, output_grad, lengths, advantage, span_plan)


def solution(mesh):
    return jax.shard_map(
        local,
        mesh=mesh,
        in_specs=(
            P(("dp", "ctx"), None),
            P(("dp", "ctx"), None),
            P(("dp", "ctx"), None),
            P(("dp", "ctx"), None),
            P("dp", None),
            P("dp", None),
            P("dp", None, None),
        ),
        out_specs=(P(("dp", "ctx"), None), P(("dp", "ctx"), None), P(("ctx", "dp"), None)),
        check_vma=False,
    )
```

```python
import jax
import jax.numpy as jnp
from jax import lax
from jax.experimental import pallas as pl
from jax.experimental.pallas import tpu as pltpu
from jax.sharding import PartitionSpec as P

NEG_FILL = -1e30
MESH = pl.DeviceIdType.MESH
T = 128
HQ = 4
HD = 128
SEEN = 5
FEAT = 512
SCALE = HD**-0.5
OTHERS = [(2, 0), (2, 1), (1, 0), (1, 1), (3, 0), (3, 1), (0, 1)]
VALUE, KEY = 0, 1
COLUMNS = [pl.ds(HD, HD), pl.ds(0, HD)]


def dot_nt(a, b):
    return lax.dot_general(a, b, (((1,), (1,)), ((), ())), preferred_element_type=jnp.float32)


def dot_nn(a, b):
    return lax.dot_general(a, b, (((1,), (0,)), ((), ())), preferred_element_type=jnp.float32)


def kernel(normed, query, kv, og, lengths_in, advantage_in, plan_in, qg_out, kvg_out, wg_out,
           lengths, advantage, plan, q_in, og_in, q_st, o_st, kvb, k_t, bias, p_st, ds_st, onehot, part, got, own_far, far_sum, far_got,
           q_send, q_recv, x_in, x_t, x_all, g_all, w_acc, w_send, w_got, w_z, w_z_got,
           loc_sem, kz_s, kz_r, kp_s, kp_r, kf_s, kf_r, x_s, x_r, d_s, d_r, dz_s, dz_r, qa_s, qa_r, g_s, g_r, w_s, w_r, z_s, z_r):
    d = lax.axis_index("dp")
    c = lax.axis_index("ctx")
    j, p = c // 2, c % 2
    z_lo, core = d // 2, d % 2
    z = p * 8 + z_lo
    y, x = j // 4, lax.rem(j, 4)
    own_slot = (x * 2 + core, y * 2 + core)
    own_pos = (x, y)

    def plane(offset):
        return (d, lax.rem(j + offset, 16) * 2 + p)

    partner = (d, j * 2 + (1 - p))

    def line(axis, offset, flip):
        to_core = core if flip == 0 else 1 - core
        to_x = lax.rem(x + offset, 4) if axis == 0 else x
        to_y = lax.rem(y + offset, 4) if axis == 1 else y
        return (z_lo * 2 + to_core, (to_y * 4 + to_x) * 2 + p)

    def along_z(offset):
        there = lax.rem(z + offset, 16)
        return (lax.rem(there, 8) * 2 + core, j * 2 + there // 8)

    def remote(src, dst, send, recv, where):
        return pltpu.make_async_remote_copy(src_ref=src, dst_ref=dst, send_sem=send, recv_sem=recv,
                                            device_id=where, device_id_type=MESH)

    sends, recvs = [], []

    def launch(*cps):
        for cp in cps:
            cp.start()
            sends.append(cp)
            recvs.append(cp)

    def take(*cps):
        for cp in cps:
            recvs[:] = [r for r in recvs if r is not cp]
            cp.wait_recv()

    def launch_all(make, low, high):
        def step(o, carry):
            make(o).start()
            return carry

        lax.fori_loop(low, high, step, 0)
        sends.append((make, low, high))
        recvs.append((make, low, high))

    def take_all(make, low, high, then=None):
        def step(o, carry):
            make(o).wait_recv()
            if then is not None:
                then(o)
            return carry

        recvs[:] = [r for r in recvs if not (isinstance(r, tuple) and r[0] is make and r[1:] == (low, high))]
        lax.fori_loop(low, high, step, 0)

    barrier = pltpu.get_barrier_semaphore()

    def greet_ctx(o, carry):
        pl.semaphore_signal(barrier, inc=1, device_id=(d, lax.rem(c + o, 32)), device_id_type=MESH)
        return carry

    def greet_z(o, carry):
        pl.semaphore_signal(barrier, inc=1, device_id=along_z(o), device_id_type=MESH)
        return carry

    lax.fori_loop(1, 32, greet_ctx, 0)
    lax.fori_loop(1, 8, greet_z, 0)
    lax.fori_loop(9, 16, greet_z, 0)
    for axis, offset in [(0, 0), (0, 1), (0, 2), (0, 3), (1, 1), (1, 2), (1, 3)]:
        pl.semaphore_signal(barrier, inc=1, device_id=line(axis, offset, 1), device_id_type=MESH)
    loads = [
        pltpu.make_async_copy(query, q_in, loc_sem.at[0]),
        pltpu.make_async_copy(og, og_in, loc_sem.at[1]),
        pltpu.make_async_copy(kv, kvb.at[0], loc_sem.at[2]),
        pltpu.make_async_copy(normed, x_in, loc_sem.at[3]),
        pltpu.make_async_copy(lengths_in, lengths, loc_sem.at[4]),
        pltpu.make_async_copy(advantage_in, advantage, loc_sem.at[5]),
        pltpu.make_async_copy(plan_in.at[0], plan, loc_sem.at[6]),
    ]
    for cp in loads:
        cp.start()

    pl.semaphore_wait(barrier, 52)

    halves = [pl.ds(0, HD), pl.ds(HD, HD)]
    kz = [remote(kv.at[:, half], kvb.at[SEEN, :, half], kz_s.at[i], kz_r.at[i], partner) for i, half in enumerate(halves)]
    launch(*kz)
    kp = [remote(kv, kvb.at[o], kp_s.at[o - 1], kp_r.at[o - 1], plane(o)) for o in range(1, SEEN)]
    launch(*kp)

    loads[3].wait()

    def turn(at, carry):
        for q in range(4):
            block = x_in[:, pl.ds(pl.multiple_of(at * FEAT + q * T, T), T)].T
            for low in range(4):
                for k in range(2):
                    x_t[q // 2, k, at // 4, lax.rem(at, 4), pl.ds(((q % 2) * 4 + low) * 16, 16), :] = (
                        block[(low * 2 + k) * 16 : (low * 2 + k + 1) * 16])
        return carry

    lax.fori_loop(0, 16, turn, 0)

    def x_source(axis, offset, flip):
        to_core = core if flip == 0 else 1 - core
        if axis == 0:
            return x_t.at[0, to_core, :, lax.rem(x + offset, 4)]
        return x_t.at[1, to_core, lax.rem(y + offset, 4)]

    def x_place(axis):
        return x_all.at[axis, :, :, pl.ds(pl.multiple_of(own_slot[axis] * T, T), T)]

    x_copies = {}
    for axis in range(2):
        for offset, flip in OTHERS:
            m = axis * 7 + offset * 2 + flip - 1
            x_copies[axis, offset, flip] = remote(x_source(axis, offset, flip), x_place(axis), x_s.at[m], x_r.at[m], line(axis, offset, flip))
    x_own = [pltpu.make_async_copy(x_source(axis, 0, 0), x_place(axis), loc_sem.at[7 + axis]) for axis in range(2)]
    for cp in x_own:
        cp.start()
    launch(*[cp for (axis, offset, flip), cp in x_copies.items() if offset != 2])

    for cp in loads[4:]:
        cp.wait()
    lanes = lax.broadcasted_iota(jnp.int32, (1, T), 1)
    rows = lax.broadcasted_iota(jnp.int32, (T, HD), 0)
    pos_lane = c * T + lanes
    pos_row = c * T + rows
    start_lane = jnp.zeros((1, T), jnp.int32)
    adv_row = jnp.zeros((T, HD), jnp.float32)
    end = jnp.int32(0)
    for i in range(16):
        begin = end
        end = end + lengths[0, i]
        start_lane = jnp.where(pos_lane >= begin, begin, start_lane)
        adv_row = jnp.where(pos_row >= begin, advantage[0, i], adv_row)
    key_rows = lax.broadcasted_iota(jnp.int32, (T, T), 0)
    for rel in range(2):
        for o in range(SEEN):
            key_plane = p if rel == 0 else 1 - p
            base = ((j - o) * 2 + key_plane) * T
            seen = (key_rows >= start_lane - base) & (key_rows <= pos_lane - base)
            bias[pl.ds((rel * SEEN + o) * T, T), :] = jnp.where(seen, 0.0, NEG_FILL)

    loads[0].wait()
    loads[1].wait()
    for h in range(HQ):
        cols = pl.ds(h * HD, HD)
        q_st[pl.ds(h * T, T), :] = q_in[:, cols]
        o_st[pl.ds(h * T, T), :] = (adv_row * og_in[:, cols].astype(jnp.float32)).astype(jnp.bfloat16)

    kf = []
    for i, half in enumerate(halves):
        take(kz[i])
        for o in range(1, SEEN):
            cp = remote(kvb.at[SEEN, :, half], kvb.at[SEEN + o, :, half], kf_s.at[i * 4 + o - 1], kf_r.at[i * 4 + o - 1], plane(o))
            launch(cp)
            kf.append(cp)
    plan_row = plan[pl.ds(c, 1), :]
    out_row = lax.broadcasted_iota(jnp.int32, (4 * T, 32), 0)
    span_no = lax.broadcasted_iota(jnp.int32, (4 * T, 32), 1)
    block = jnp.sum(jnp.where(out_row // 16 == span_no, jnp.broadcast_to(plan_row, (4 * T, 32)), 0), axis=1, keepdims=True)
    row_no = lax.broadcasted_iota(jnp.int32, (4 * T, 1), 0)
    source = (row_no // 4 % 4) * T + block * 4 + row_no % 4
    for h in range(HQ):
        col_no = lax.broadcasted_iota(jnp.int32, (4 * T, T), 1) + h * T
        onehot[:, pl.ds(h * T, T)] = jnp.where(col_no == source, 1.0, 0.0).astype(jnp.bfloat16)

    loads[2].wait()
    take(*kp)
    take(*kf)

    n_keys = 2 * SEEN * T
    keys = kvb[:, :, :HD].reshape(n_keys, HD)
    values = kvb[:, :, HD:].reshape(n_keys, HD)
    for s in range(2 * SEEN):
        k_t[:, pl.ds(s * T, T)] = kvb[s, :, :HD].T
    for h in range(HQ):
        heads = pl.ds(h * T, T)
        scores = dot_nt(keys, q_st[heads, :]) * SCALE + bias[...]
        top = jnp.max(scores, axis=0, keepdims=True)
        weights = jnp.exp(scores - top)
        probs = weights * (1.0 / jnp.sum(weights, axis=0, keepdims=True))
        grad_prob = dot_nt(values, o_st[heads, :])
        row_dot = jnp.sum(probs * grad_prob, axis=0, keepdims=True)
        ds_st[:, heads] = (probs * (grad_prob - row_dot)).astype(jnp.bfloat16)
        p_st[:, heads] = probs.astype(jnp.bfloat16)

    half_rows = SEEN * T

    def term(rel, half):
        at = pl.ds(rel * half_rows, half_rows)
        if half == VALUE:
            return dot_nn(p_st[at, :], o_st[...])
        return dot_nn(ds_st[at, :], q_st[...]) * SCALE

    sent = {}
    for rel in (1, 0):
        for half in (VALUE, KEY):
            terms = term(rel, half)
            own_far[half, rel] = terms[:T]
            part[half, pl.ds(rel * 4, 4)] = terms[T:].astype(jnp.bfloat16).reshape(SEEN - 1, T, HD)
            sent[rel, half] = []
            for o in range(1, SEEN):
                i = rel * 4 + o - 1
                cp = remote(part.at[half, i], got.at[half, i], d_s.at[half, i], d_r.at[half, i], plane(16 - o))
                launch(cp)
                sent[rel, half].append(cp)

    q_grad_t = (dot_nn(k_t[...], ds_st[...]) * SCALE).astype(jnp.bfloat16)
    q_send[...] = dot_nt(onehot[...], q_grad_t).astype(jnp.bfloat16).reshape(32, 16, HD)
    q_recv[c] = q_send[c]

    def terms_sum(rel, half):
        take(*sent[rel, half])
        total = own_far[half, rel]
        for o in range(SEEN - 1):
            total = total + got[half, rel * 4 + o].astype(jnp.float32)
        return total

    dz = []
    for half in (VALUE, KEY):
        far_sum[half] = terms_sum(1, half).astype(jnp.bfloat16)
        dz.append(remote(far_sum.at[half], far_got.at[half], dz_s.at[half], dz_r.at[half], partner))
        launch(dz[half])
    launch(*[cp for (axis, offset, flip), cp in x_copies.items() if offset == 2])
    def q_copy(o):
        there = lax.rem(c + o, 32)
        return remote(q_send.at[there], q_recv.at[c], qa_s.at[o - 1], qa_r.at[o - 1], (d, there))

    launch_all(q_copy, 1, 32)

    near = [terms_sum(0, half) for half in (VALUE, KEY)]

    g_copies = {}
    for half in (VALUE, KEY):
        take(dz[half])
        kvg = (near[half] + far_got[half].astype(jnp.float32)).astype(jnp.bfloat16)
        kvg_out[:, COLUMNS[half]] = kvg
        for axis in range(2):
            g_all[half, axis, own_slot[axis]] = kvg
        for axis in range(2):
            g_copies[half, axis] = []
            for offset, flip in OTHERS:
                m = axis * 7 + offset * 2 + flip - 1
                slot = g_all.at[half, axis, own_slot[axis]]
                cp = remote(slot, slot, g_s.at[half, m], g_r.at[half, m], line(axis, offset, flip))
                launch(cp)
                g_copies[half, axis].append(cp)

    take(*x_copies.values())
    for cp in x_own:
        cp.wait()

    w_copies = {}
    for half in (VALUE, KEY):
        for axis in range(2):
            take(*g_copies[half, axis])
            terms = dot_nn(x_all[axis].reshape(4 * T, 8 * T), g_all[half, axis].reshape(8 * T, HD)).reshape(4, T, HD)
            w_acc[half, axis] = terms
            w_send[half, axis] = terms.astype(jnp.bfloat16)
            w_copies[half, axis] = []
            for offset in (2, 1, 3):
                m = axis * 3 + offset - 1
                there = lax.rem(own_pos[1 - axis] + offset, 4)
                cp = remote(w_send.at[half, axis, there], w_got.at[half, m], w_s.at[half, m], w_r.at[half, m], line(1 - axis, offset, 0))
                launch(cp)
                w_copies[half, axis].append(cp)

    z_copies = []
    for half in (VALUE, KEY):
        for axis in range(2):
            take(*w_copies[half, axis])
            total = w_acc[half, axis, own_pos[1 - axis]]
            for offset in range(1, 4):
                total = total + w_got[half, axis * 3 + offset - 1].astype(jnp.float32)
            w_z[half, pl.ds(axis * 8, 8)] = total.astype(jnp.bfloat16).reshape(8, 16, HD)
        w_z_got[half, z] = w_z[half, z]

        def z_copy(o, half=half):
            return remote(w_z.at[half, lax.rem(z + o, 16)], w_z_got.at[half, z], z_s.at[half, o - 1], z_r.at[half, o - 1], along_z(o))

        launch_all(z_copy, 1, 16)
        z_copies.append(z_copy)

    take_all(q_copy, 1, 32)
    arrived = q_recv[...].reshape(4 * T, HD)
    tok = lax.broadcasted_iota(jnp.int32, (T, 4 * T), 0)
    place = lax.broadcasted_iota(jnp.int32, (T, 4 * T), 1)
    for h in range(HQ):
        pick = jnp.where(place == tok // 4 * 16 + h * 4 + tok % 4, 1.0, 0.0).astype(jnp.bfloat16)
        qg_out[:, pl.ds(h * HD, HD)] = dot_nn(pick, arrived).astype(jnp.bfloat16)

    for half in (VALUE, KEY):
        take_all(z_copies[half], 1, 16)
        total = jnp.sum(w_z_got[half].astype(jnp.float32), axis=0)
        wg_out[:, COLUMNS[half]] = (total * (1.0 / 256.0)).astype(jnp.bfloat16)

    for item in sends:
        if isinstance(item, tuple):
            make, low, high = item

            def step(o, carry, make=make):
                make(o).wait_send()
                return carry

            lax.fori_loop(low, high, step, 0)
        else:
            item.wait_send()

def local(normed, query, key_value, output_grad, lengths, advantage, span_plan):
    bf16, f32 = jnp.bfloat16, jnp.float32
    n_keys = 2 * SEEN * T
    dma = pltpu.SemaphoreType.DMA
    vmem = pl.BlockSpec(memory_space=pltpu.VMEM)
    return pl.pallas_call(
        kernel,
        out_shape=(
            jax.ShapeDtypeStruct((T, HQ * HD), bf16),
            jax.ShapeDtypeStruct((T, 2 * HD), bf16),
            jax.ShapeDtypeStruct((16, 2 * HD), bf16),
        ),
        in_specs=[pl.BlockSpec(memory_space=pltpu.HBM)] * 7,
        out_specs=(vmem, vmem, vmem),
        scratch_shapes=[
            pltpu.SMEM((1, 16), jnp.int32),
            pltpu.SMEM((1, 16), f32),
            pltpu.VMEM((32, 32), jnp.int32),
            pltpu.VMEM((T, HQ * HD), bf16),
            pltpu.VMEM((T, HQ * HD), bf16),
            pltpu.VMEM((HQ * T, HD), bf16),
            pltpu.VMEM((HQ * T, HD), bf16),
            pltpu.VMEM((2 * SEEN, T, 2 * HD), bf16),
            pltpu.VMEM((HD, n_keys), bf16),
            pltpu.VMEM((n_keys, T), f32),
            pltpu.VMEM((n_keys, HQ * T), bf16),
            pltpu.VMEM((n_keys, HQ * T), bf16),
            pltpu.VMEM((HQ * T, HQ * T), bf16),
            pltpu.VMEM((2, 8, T, HD), bf16),
            pltpu.VMEM((2, 8, T, HD), bf16),
            pltpu.VMEM((2, 2, T, HD), f32),
            pltpu.VMEM((2, T, HD), bf16),
            pltpu.VMEM((2, T, HD), bf16),
            pltpu.VMEM((32, 16, HD), bf16),
            pltpu.VMEM((32, 16, HD), bf16),
            pltpu.VMEM((T, 16 * FEAT), bf16),
            pltpu.VMEM((2, 2, 4, 4, T, T), bf16),
            pltpu.VMEM((2, 4, T, 8 * T), bf16),
            pltpu.VMEM((2, 2, 8, T, HD), bf16),
            pltpu.VMEM((2, 2, 4, T, HD), f32),
            pltpu.VMEM((2, 2, 4, T, HD), bf16),
            pltpu.VMEM((2, 6, T, HD), bf16),
            pltpu.VMEM((2, 16, 16, HD), bf16),
            pltpu.VMEM((2, 16, 16, HD), bf16),
            dma((9,)), dma((2,)), dma((2,)), dma((4,)), dma((4,)), dma((8,)), dma((8,)),
            dma((14,)), dma((14,)), dma((2, 8)), dma((2, 8)), dma((2,)), dma((2,)), dma((31,)), dma((31,)),
            dma((2, 14)), dma((2, 14)), dma((2, 6)), dma((2, 6)), dma((2, 15)), dma((2, 15)),
        ],
        compiler_params=pltpu.CompilerParams(collective_id=0, has_side_effects=True, vmem_limit_bytes=48 * 2**20),
        name="backward",
    )(*[pltpu.with_memory_space_constraint(a, pltpu.HBM) for a in (normed, query, key_value, output_grad, lengths, advantage, span_plan)])


def solution(mesh):
    return jax.shard_map(
        local,
        mesh=mesh,
        in_specs=(
            P(("dp", "ctx"), None),
            P(("dp", "ctx"), None),
            P(("dp", "ctx"), None),
            P(("dp", "ctx"), None),
            P("dp", None),
            P("dp", None),
            P("dp", None, None),
        ),
        out_specs=(P(("dp", "ctx"), None), P(("dp", "ctx"), None), P(("ctx", "dp"), None)),
        check_vma=False,
    )
```

```python
import jax
import jax.numpy as jnp
from jax import lax
from jax.experimental import pallas as pl
from jax.experimental.pallas import tpu as pltpu
from jax.sharding import PartitionSpec as P

NEG_FILL = -1e30
MESH = pl.DeviceIdType.MESH
T = 128
HQ = 4
HD = 128
SEEN = 5
FEAT = 512
SCALE = HD**-0.5
OTHERS = [(2, 0), (2, 1), (1, 0), (1, 1), (3, 0), (3, 1), (0, 1)]
VALUE, KEY = 0, 1
COLUMNS = [pl.ds(HD, HD), pl.ds(0, HD)]


def dot_nt(a, b):
    return lax.dot_general(a, b, (((1,), (1,)), ((), ())), preferred_element_type=jnp.float32)


def dot_nn(a, b):
    return lax.dot_general(a, b, (((1,), (0,)), ((), ())), preferred_element_type=jnp.float32)


def kernel(normed, query, kv, og, lengths_in, advantage_in, plan_in, qg_out, kvg_out, wg_out,
           lengths, advantage, plan, q_in, og_in, q_st, o_st, kvb, k_t, bias, score, grad_prob, p_st, ds_st, onehot, part, got, own_far, far_sum, far_got,
           q_send, q_recv, x_in, x_t, x_all, g_all, w_acc, w_send, w_got, w_z, w_z_got,
           loc_sem, kz_s, kz_r, kp_s, kp_r, kf_s, kf_r, x_s, x_r, d_s, d_r, dz_s, dz_r, qa_s, qa_r, g_s, g_r, w_s, w_r, z_s, z_r):
    d = lax.axis_index("dp")
    c = lax.axis_index("ctx")
    j, p = c // 2, c % 2
    z_lo, core = d // 2, d % 2
    z = p * 8 + z_lo
    y, x = j // 4, lax.rem(j, 4)
    own_slot = (x * 2 + core, y * 2 + core)
    own_pos = (x, y)

    def plane(offset):
        return (d, lax.rem(j + offset, 16) * 2 + p)

    partner = (d, j * 2 + (1 - p))

    def line(axis, offset, flip):
        to_core = core if flip == 0 else 1 - core
        to_x = lax.rem(x + offset, 4) if axis == 0 else x
        to_y = lax.rem(y + offset, 4) if axis == 1 else y
        return (z_lo * 2 + to_core, (to_y * 4 + to_x) * 2 + p)

    def along_z(offset):
        there = lax.rem(z + offset, 16)
        return (lax.rem(there, 8) * 2 + core, j * 2 + there // 8)

    def remote(src, dst, send, recv, where):
        return pltpu.make_async_remote_copy(src_ref=src, dst_ref=dst, send_sem=send, recv_sem=recv,
                                            device_id=where, device_id_type=MESH)

    sends = []

    def whole(ref, send, recv):
        return remote(ref, ref, send, recv, partner)

    def start(cps, group):
        for cp in cps:
            cp.start()
        sends.append(group)

    def start_all(make, low, high):
        def step(o, carry):
            make(o).start()
            return carry

        lax.fori_loop(low, high, step, 0)

    def drain(items):
        for cp in items:
            cp.wait_send()

    barrier = pltpu.get_barrier_semaphore()

    def greet_far(o, carry):
        there = lax.rem(j + o, 16) * 2 + (1 - p)
        pl.semaphore_signal(barrier, inc=1, device_id=(d, there), device_id_type=MESH)
        return carry

    def greet_plane(o, carry):
        pl.semaphore_signal(barrier, inc=1, device_id=plane(o), device_id_type=MESH)
        return carry

    def greet_z(o, carry):
        pl.semaphore_signal(barrier, inc=1, device_id=along_z(o), device_id_type=MESH)
        return carry

    lax.fori_loop(0, 16, greet_far, 0)
    lax.fori_loop(1, 8, greet_z, 0)
    lax.fori_loop(9, 16, greet_z, 0)
    lax.fori_loop(1, 16, greet_plane, 0)
    for axis, offset in [(0, 0), (0, 1), (0, 2), (0, 3), (1, 1), (1, 2), (1, 3)]:
        pl.semaphore_signal(barrier, inc=1, device_id=line(axis, offset, 1), device_id_type=MESH)
    loads = [
        pltpu.make_async_copy(query, q_in, loc_sem.at[0]),
        pltpu.make_async_copy(og, og_in, loc_sem.at[1]),
        pltpu.make_async_copy(kv, kvb.at[0], loc_sem.at[2]),
        pltpu.make_async_copy(normed, x_in, loc_sem.at[3]),
        pltpu.make_async_copy(lengths_in, lengths, loc_sem.at[4]),
        pltpu.make_async_copy(advantage_in, advantage, loc_sem.at[5]),
        pltpu.make_async_copy(plan_in.at[0], plan, loc_sem.at[6]),
    ]
    for cp in loads:
        cp.start()

    pl.semaphore_wait(barrier, 52)

    halves = [pl.ds(0, HD), pl.ds(HD, HD)]
    kz = [remote(kv.at[:, half], kvb.at[SEEN, :, half], kz_s.at[i], kz_r.at[i], partner) for i, half in enumerate(halves)]
    for cp in kz:
        start([cp], cp)
    kp = [remote(kv, kvb.at[o], kp_s, kp_r, plane(o)) for o in range(1, SEEN)]
    kp_whole = whole(kvb.at[pl.ds(0, SEEN - 1)], kp_s, kp_r)
    start(kp, kp_whole)

    loads[3].wait()

    def turn(at, carry):
        for q in range(4):
            block = x_in[:, pl.ds(pl.multiple_of(at * FEAT + q * T, T), T)].T
            for low in range(4):
                for k in range(2):
                    x_t[q // 2, k, at // 4, lax.rem(at, 4), pl.ds(((q % 2) * 4 + low) * 16, 16), :] = (
                        block[(low * 2 + k) * 16 : (low * 2 + k + 1) * 16])
        return carry

    lax.fori_loop(0, 16, turn, 0)

    def x_source(axis, offset, flip):
        to_core = core if flip == 0 else 1 - core
        if axis == 0:
            return x_t.at[0, to_core, :, lax.rem(x + offset, 4)]
        return x_t.at[1, to_core, lax.rem(y + offset, 4)]

    def x_place(axis):
        return x_all.at[axis, :, :, pl.ds(pl.multiple_of(own_slot[axis] * T, T), T)]

    x_copies = {}
    for axis in range(2):
        for offset, flip in OTHERS:
            x_copies[axis, offset, flip] = remote(x_source(axis, offset, flip), x_place(axis), x_s.at[axis], x_r.at[axis], line(axis, offset, flip))
    x_own = [pltpu.make_async_copy(x_source(axis, 0, 0), x_place(axis), loc_sem.at[7 + axis]) for axis in range(2)]
    for cp in x_own:
        cp.start()

    for cp in loads[4:]:
        cp.wait()
    lanes = lax.broadcasted_iota(jnp.int32, (1, T), 1)
    rows = lax.broadcasted_iota(jnp.int32, (T, HD), 0)
    pos_lane = c * T + lanes
    pos_row = c * T + rows
    start_lane = jnp.zeros((1, T), jnp.int32)
    adv_row = jnp.zeros((T, HD), jnp.float32)
    end = jnp.int32(0)
    for i in range(16):
        begin = end
        end = end + lengths[0, i]
        start_lane = jnp.where(pos_lane >= begin, begin, start_lane)
        adv_row = jnp.where(pos_row >= begin, advantage[0, i], adv_row)
    key_rows = lax.broadcasted_iota(jnp.int32, (T, T), 0)
    for rel in range(2):
        for o in range(SEEN):
            key_plane = p if rel == 0 else 1 - p
            base = ((j - o) * 2 + key_plane) * T
            seen = (key_rows >= start_lane - base) & (key_rows <= pos_lane - base)
            bias[pl.ds((rel * SEEN + o) * T, T), :] = jnp.where(seen, 0.0, NEG_FILL)

    loads[0].wait()
    loads[1].wait()
    for h in range(HQ):
        cols = pl.ds(h * HD, HD)
        q_st[pl.ds(h * T, T), :] = q_in[:, cols]
        o_st[pl.ds(h * T, T), :] = (adv_row * og_in[:, cols].astype(jnp.float32)).astype(jnp.bfloat16)

    kf = []
    for i, half in enumerate(halves):
        kz[i].wait_recv()
        cps = [remote(kvb.at[SEEN, :, half], kvb.at[SEEN + o, :, half], kf_s.at[i], kf_r.at[i], plane(o)) for o in range(1, SEEN)]
        kf.append(whole(kvb.at[pl.ds(0, SEEN - 1), :, half], kf_s.at[i], kf_r.at[i]))
        start(cps, kf[i])
    for (axis, offset, flip), cp in x_copies.items():
        if offset != 2:
            cp.start()

    half_rows = SEEN * T

    def scores_of(rel):
        at = pl.ds(rel * half_rows, half_rows)
        keys = kvb[pl.ds(rel * SEEN, SEEN), :, :HD].reshape(half_rows, HD)
        values = kvb[pl.ds(rel * SEEN, SEEN), :, HD:].reshape(half_rows, HD)
        for h in range(HQ):
            heads = pl.ds(h * T, T)
            score[at, heads] = dot_nt(keys, q_st[heads, :]) * SCALE + bias[at, :]
            grad_prob[at, heads] = dot_nt(values, o_st[heads, :])

    loads[2].wait()
    kp_whole.wait_recv()
    scores_of(0)
    for group in kf:
        group.wait_recv()
    scores_of(1)
    for h in range(HQ):
        heads = pl.ds(h * T, T)
        scores = score[:, heads]
        weights = jnp.exp(scores - jnp.max(scores, axis=0, keepdims=True))
        probs = weights * (1.0 / jnp.sum(weights, axis=0, keepdims=True))
        row_dot = jnp.sum(probs * grad_prob[:, heads], axis=0, keepdims=True)
        ds_st[:, heads] = (probs * (grad_prob[:, heads] - row_dot)).astype(jnp.bfloat16)
        p_st[:, heads] = probs.astype(jnp.bfloat16)

    def term(rel, half):
        at = pl.ds(rel * half_rows, half_rows)
        if half == VALUE:
            return dot_nn(p_st[at, :], o_st[...])
        return dot_nn(ds_st[at, :], q_st[...]) * SCALE

    sent = {}
    for rel in (1, 0):
        for half in (VALUE, KEY):
            terms = term(rel, half)
            own_far[half, rel] = terms[:T]
            part[half, pl.ds(rel * 4, 4)] = terms[T:].astype(jnp.bfloat16).reshape(SEEN - 1, T, HD)
            at = pl.ds(rel * 4, 4)
            send, recv = d_s.at[half, rel], d_r.at[half, rel]
            cps = [remote(part.at[half, rel * 4 + o - 1], got.at[half, rel * 4 + o - 1], send, recv, plane(16 - o)) for o in range(1, SEEN)]
            sent[rel, half] = whole(got.at[half, at], send, recv)
            start(cps, sent[rel, half])

    def terms_sum(rel, half):
        sent[rel, half].wait_recv()
        total = own_far[half, rel]
        for o in range(SEEN - 1):
            total = total + got[half, rel * 4 + o].astype(jnp.float32)
        return total

    dz = []
    for half in (VALUE, KEY):
        far_sum[half] = terms_sum(1, half).astype(jnp.bfloat16)
        dz.append(remote(far_sum.at[half], far_got.at[half], dz_s.at[half], dz_r.at[half], partner))
        start([dz[half]], dz[half])
    for (axis, offset, flip), cp in x_copies.items():
        if offset == 2:
            cp.start()
    x_whole = [whole(x_all.at[axis, :, :, pl.ds(0, 7 * T)], x_s.at[axis], x_r.at[axis]) for axis in range(2)]
    sends.extend(x_whole)
    plan_row = plan[pl.ds(c, 1), :]
    out_row = lax.broadcasted_iota(jnp.int32, (4 * T, 32), 0)
    span_no = lax.broadcasted_iota(jnp.int32, (4 * T, 32), 1)
    block = jnp.sum(jnp.where(out_row // 16 == span_no, jnp.broadcast_to(plan_row, (4 * T, 32)), 0), axis=1, keepdims=True)
    row_no = lax.broadcasted_iota(jnp.int32, (4 * T, 1), 0)
    source = (row_no // 4 % 4) * T + block * 4 + row_no % 4
    for h in range(HQ):
        col_no = lax.broadcasted_iota(jnp.int32, (4 * T, T), 1) + h * T
        onehot[:, pl.ds(h * T, T)] = jnp.where(col_no == source, 1.0, 0.0).astype(jnp.bfloat16)


    for s in range(2 * SEEN):
        k_t[:, pl.ds(s * T, T)] = kvb[s, :, :HD].T
    q_grad_t = (dot_nn(k_t[...], ds_st[...]) * SCALE).astype(jnp.bfloat16)
    q_send[...] = dot_nt(onehot[...], q_grad_t).astype(jnp.bfloat16).reshape(32, 16, HD)
    q_recv[c] = q_send[c]

    def q_copy(o):
        there = lax.rem(c + o, 32)
        return remote(q_send.at[there], q_recv.at[c], qa_s, qa_r, (d, there))

    q_whole = whole(q_recv.at[pl.ds(0, 31)], qa_s, qa_r)

    start_all(q_copy, 1, 32)
    sends.append(q_whole)

    near = [terms_sum(0, half) for half in (VALUE, KEY)]

    g_copies = {}
    for half in (VALUE, KEY):
        dz[half].wait_recv()
        kvg = (near[half] + far_got[half].astype(jnp.float32)).astype(jnp.bfloat16)
        kvg_out[:, COLUMNS[half]] = kvg
        for axis in range(2):
            g_all[half, axis, own_slot[axis]] = kvg
        for axis in range(2):
            slot = g_all.at[half, axis, own_slot[axis]]
            send, recv = g_s.at[half, axis], g_r.at[half, axis]
            g_copies[half, axis] = whole(g_all.at[half, axis, pl.ds(0, 7)], send, recv)
            start([remote(slot, slot, send, recv, line(axis, offset, flip)) for offset, flip in OTHERS], g_copies[half, axis])

    for axis in range(2):
        x_whole[axis].wait_recv()
        x_own[axis].wait()

    w_copies = {}
    for half in (VALUE, KEY):
        for axis in range(2):
            g_copies[half, axis].wait_recv()
            terms = dot_nn(x_all[axis].reshape(4 * T, 8 * T), g_all[half, axis].reshape(8 * T, HD)).reshape(4, T, HD)
            w_acc[half, axis] = terms
            w_send[half, axis] = terms.astype(jnp.bfloat16)
            send, recv = w_s.at[half, axis], w_r.at[half, axis]
            cps = []
            for offset in (2, 1, 3):
                there = lax.rem(own_pos[1 - axis] + offset, 4)
                cps.append(remote(w_send.at[half, axis, there], w_got.at[half, axis * 3 + offset - 1], send, recv, line(1 - axis, offset, 0)))
            w_copies[half, axis] = whole(w_got.at[half, pl.ds(axis * 3, 3)], send, recv)
            start(cps, w_copies[half, axis])

    z_copies = []
    for half in (VALUE, KEY):
        for axis in range(2):
            w_copies[half, axis].wait_recv()
            total = w_acc[half, axis, own_pos[1 - axis]]
            for offset in range(1, 4):
                total = total + w_got[half, axis * 3 + offset - 1].astype(jnp.float32)
            w_z[half, pl.ds(axis * 8, 8)] = total.astype(jnp.bfloat16).reshape(8, 16, HD)
        w_z_got[half, z] = w_z[half, z]

        def z_copy(o, half=half):
            return remote(w_z.at[half, lax.rem(z + o, 16)], w_z_got.at[half, z], z_s.at[half], z_r.at[half], along_z(o))

        start_all(z_copy, 1, 16)
        z_copies.append(whole(w_z_got.at[half, pl.ds(0, 15)], z_s.at[half], z_r.at[half]))

    q_whole.wait_recv()
    arrived = q_recv[...].reshape(4 * T, HD)
    tok = lax.broadcasted_iota(jnp.int32, (T, 4 * T), 0)
    place = lax.broadcasted_iota(jnp.int32, (T, 4 * T), 1)
    for h in range(HQ):
        pick = jnp.where(place == tok // 4 * 16 + h * 4 + tok % 4, 1.0, 0.0).astype(jnp.bfloat16)
        qg_out[:, pl.ds(h * HD, HD)] = dot_nn(pick, arrived).astype(jnp.bfloat16)

    drain(sends)
    for half in (VALUE, KEY):
        z_copies[half].wait_recv()
        total = jnp.sum(w_z_got[half].astype(jnp.float32), axis=0)
        wg_out[:, COLUMNS[half]] = (total * (1.0 / 256.0)).astype(jnp.bfloat16)
    drain(z_copies)


def local(normed, query, key_value, output_grad, lengths, advantage, span_plan):
    bf16, f32 = jnp.bfloat16, jnp.float32
    n_keys = 2 * SEEN * T
    dma = pltpu.SemaphoreType.DMA
    vmem = pl.BlockSpec(memory_space=pltpu.VMEM)
    return pl.pallas_call(
        kernel,
        out_shape=(
            jax.ShapeDtypeStruct((T, HQ * HD), bf16),
            jax.ShapeDtypeStruct((T, 2 * HD), bf16),
            jax.ShapeDtypeStruct((16, 2 * HD), bf16),
        ),
        in_specs=[pl.BlockSpec(memory_space=pltpu.HBM)] * 7,
        out_specs=(vmem, vmem, vmem),
        scratch_shapes=[
            pltpu.SMEM((1, 16), jnp.int32),
            pltpu.SMEM((1, 16), f32),
            pltpu.VMEM((32, 32), jnp.int32),
            pltpu.VMEM((T, HQ * HD), bf16),
            pltpu.VMEM((T, HQ * HD), bf16),
            pltpu.VMEM((HQ * T, HD), bf16),
            pltpu.VMEM((HQ * T, HD), bf16),
            pltpu.VMEM((2 * SEEN, T, 2 * HD), bf16),
            pltpu.VMEM((HD, n_keys), bf16),
            pltpu.VMEM((n_keys, T), f32),
            pltpu.VMEM((n_keys, HQ * T), f32),
            pltpu.VMEM((n_keys, HQ * T), f32),
            pltpu.VMEM((n_keys, HQ * T), bf16),
            pltpu.VMEM((n_keys, HQ * T), bf16),
            pltpu.VMEM((HQ * T, HQ * T), bf16),
            pltpu.VMEM((2, 8, T, HD), bf16),
            pltpu.VMEM((2, 8, T, HD), bf16),
            pltpu.VMEM((2, 2, T, HD), f32),
            pltpu.VMEM((2, T, HD), bf16),
            pltpu.VMEM((2, T, HD), bf16),
            pltpu.VMEM((32, 16, HD), bf16),
            pltpu.VMEM((32, 16, HD), bf16),
            pltpu.VMEM((T, 16 * FEAT), bf16),
            pltpu.VMEM((2, 2, 4, 4, T, T), bf16),
            pltpu.VMEM((2, 4, T, 8 * T), bf16),
            pltpu.VMEM((2, 2, 8, T, HD), bf16),
            pltpu.VMEM((2, 2, 4, T, HD), f32),
            pltpu.VMEM((2, 2, 4, T, HD), bf16),
            pltpu.VMEM((2, 6, T, HD), bf16),
            pltpu.VMEM((2, 16, 16, HD), bf16),
            pltpu.VMEM((2, 16, 16, HD), bf16),
            dma((9,)), dma((2,)), dma((2,)), dma, dma, dma((2,)), dma((2,)),
            dma((2,)), dma((2,)), dma((2, 2)), dma((2, 2)), dma((2,)), dma((2,)), dma, dma,
            dma((2, 2)), dma((2, 2)), dma((2, 2)), dma((2, 2)), dma((2,)), dma((2,)),
        ],
        compiler_params=pltpu.CompilerParams(collective_id=0, has_side_effects=True, vmem_limit_bytes=48 * 2**20),
        name="backward",
    )(*[pltpu.with_memory_space_constraint(a, pltpu.HBM) for a in (normed, query, key_value, output_grad, lengths, advantage, span_plan)])


def solution(mesh):
    return jax.shard_map(
        local,
        mesh=mesh,
        in_specs=(
            P(("dp", "ctx"), None),
            P(("dp", "ctx"), None),
            P(("dp", "ctx"), None),
            P(("dp", "ctx"), None),
            P("dp", None),
            P("dp", None),
            P("dp", None, None),
        ),
        out_specs=(P(("dp", "ctx"), None), P(("dp", "ctx"), None), P(("ctx", "dp"), None)),
        check_vma=False,
    )
```

```python
import jax
import jax.numpy as jnp
from jax import lax
from jax.experimental import pallas as pl
from jax.experimental.pallas import tpu as pltpu
from jax.sharding import PartitionSpec as P

NEG_FILL = -1e30
MESH = pl.DeviceIdType.MESH
T = 128
HQ = 4
HD = 128
SEEN = 5
FEAT = 512
SCALE = HD**-0.5
OTHERS = [(2, 0), (2, 1), (1, 0), (1, 1), (3, 0), (3, 1), (0, 1)]
VALUE, KEY = 0, 1
COLUMNS = [pl.ds(HD, HD), pl.ds(0, HD)]


def dot_nt(a, b):
    return lax.dot_general(a, b, (((1,), (1,)), ((), ())), preferred_element_type=jnp.float32)


def dot_nn(a, b):
    return lax.dot_general(a, b, (((1,), (0,)), ((), ())), preferred_element_type=jnp.float32)


def kernel(normed, query, kv, og, lengths_in, advantage_in, plan_in, qg_out, kvg_out, wg_out,
           lengths, advantage, plan, q_in, og_in, q_st, o_st, kvb, k_t, bias, score, grad_prob, p_st, ds_st, onehot, part, got, own_far, far_sum, far_got,
           q_send, q_recv, x_in, x_t, x_all, g_all, w_acc, w_send, w_got, w_z, w_z_got,
           loc_sem, kz_s, kz_r, kp_s, kp_r, kf_s, kf_r, x_s, x_r, d_s, d_r, dz_s, dz_r, qa_s, qa_r, g_s, g_r, w_s, w_r, z_s, z_r):
    d = lax.axis_index("dp")
    c = lax.axis_index("ctx")
    j, p = c // 2, c % 2
    z_lo, core = d // 2, d % 2
    z = p * 8 + z_lo
    y, x = j // 4, lax.rem(j, 4)
    own_slot = (x * 2 + core, y * 2 + core)
    own_pos = (x, y)

    def plane(offset):
        return (d, lax.rem(j + offset, 16) * 2 + p)

    partner = (d, j * 2 + (1 - p))

    def line(axis, offset, flip):
        to_core = core if flip == 0 else 1 - core
        to_x = lax.rem(x + offset, 4) if axis == 0 else x
        to_y = lax.rem(y + offset, 4) if axis == 1 else y
        return (z_lo * 2 + to_core, (to_y * 4 + to_x) * 2 + p)

    def along_z(offset):
        there = lax.rem(z + offset, 16)
        return (lax.rem(there, 8) * 2 + core, j * 2 + there // 8)

    def remote(src, dst, send, recv, where):
        return pltpu.make_async_remote_copy(src_ref=src, dst_ref=dst, send_sem=send, recv_sem=recv,
                                            device_id=where, device_id_type=MESH)

    sends = []

    def whole(ref, send, recv):
        return remote(ref, ref, send, recv, partner)

    def start(cps, group):
        for cp in cps:
            cp.start()
        sends.append(group)

    def start_all(make, low, high):
        for o in range(low, high):
            make(o).start()

    def drain(items):
        for cp in items:
            cp.wait_send()

    barrier = pltpu.get_barrier_semaphore()

    def greet(where):
        pl.semaphore_signal(barrier, inc=1, device_id=where, device_id_type=MESH)

    for o in range(16):
        greet((d, lax.rem(j + o, 16) * 2 + (1 - p)))
    for o in range(1, 16):
        if o != 8:
            greet(along_z(o))
    for o in range(1, 16):
        greet(plane(o))
    for axis, offset in [(0, 0), (0, 1), (0, 2), (0, 3), (1, 1), (1, 2), (1, 3)]:
        pl.semaphore_signal(barrier, inc=1, device_id=line(axis, offset, 1), device_id_type=MESH)
    loads = [
        pltpu.make_async_copy(query, q_in, loc_sem.at[0]),
        pltpu.make_async_copy(og, og_in, loc_sem.at[1]),
        pltpu.make_async_copy(kv, kvb.at[0], loc_sem.at[2]),
        pltpu.make_async_copy(normed, x_in, loc_sem.at[3]),
        pltpu.make_async_copy(lengths_in, lengths, loc_sem.at[4]),
        pltpu.make_async_copy(advantage_in, advantage, loc_sem.at[5]),
        pltpu.make_async_copy(plan_in.at[0], plan, loc_sem.at[6]),
    ]
    for cp in loads:
        cp.start()

    pl.semaphore_wait(barrier, 52)

    halves = [pl.ds(0, HD), pl.ds(HD, HD)]
    kz = [remote(kv.at[:, half], kvb.at[SEEN, :, half], kz_s.at[i], kz_r.at[i], partner) for i, half in enumerate(halves)]
    for cp in kz:
        start([cp], cp)
    kp = [remote(kv, kvb.at[o], kp_s, kp_r, plane(o)) for o in range(1, SEEN)]
    kp_whole = whole(kvb.at[pl.ds(0, SEEN - 1)], kp_s, kp_r)
    start(kp, kp_whole)

    loads[3].wait()

    def turn(at, carry):
        for q in range(4):
            block = x_in[:, pl.ds(pl.multiple_of(at * FEAT + q * T, T), T)].T
            for low in range(4):
                for k in range(2):
                    x_t[q // 2, k, at // 4, lax.rem(at, 4), pl.ds(((q % 2) * 4 + low) * 16, 16), :] = (
                        block[(low * 2 + k) * 16 : (low * 2 + k + 1) * 16])
        return carry

    lax.fori_loop(0, 16, turn, 0)

    def x_source(axis, offset, flip):
        to_core = core if flip == 0 else 1 - core
        if axis == 0:
            return x_t.at[0, to_core, :, lax.rem(x + offset, 4)]
        return x_t.at[1, to_core, lax.rem(y + offset, 4)]

    def x_place(axis):
        return x_all.at[axis, :, :, pl.ds(pl.multiple_of(own_slot[axis] * T, T), T)]

    x_copies = {}
    for axis in range(2):
        for offset, flip in OTHERS:
            x_copies[axis, offset, flip] = remote(x_source(axis, offset, flip), x_place(axis), x_s.at[axis], x_r.at[axis], line(axis, offset, flip))
    x_own = [pltpu.make_async_copy(x_source(axis, 0, 0), x_place(axis), loc_sem.at[7 + axis]) for axis in range(2)]
    for cp in x_own:
        cp.start()

    for cp in loads[4:]:
        cp.wait()
    lanes = lax.broadcasted_iota(jnp.int32, (1, T), 1)
    rows = lax.broadcasted_iota(jnp.int32, (T, HD), 0)
    pos_lane = c * T + lanes
    pos_row = c * T + rows
    start_lane = jnp.zeros((1, T), jnp.int32)
    adv_row = jnp.zeros((T, HD), jnp.float32)
    end = jnp.int32(0)
    for i in range(16):
        begin = end
        end = end + lengths[0, i]
        start_lane = jnp.where(pos_lane >= begin, begin, start_lane)
        adv_row = jnp.where(pos_row >= begin, advantage[0, i], adv_row)
    key_rows = lax.broadcasted_iota(jnp.int32, (T, T), 0)
    for rel in range(2):
        for o in range(SEEN):
            key_plane = p if rel == 0 else 1 - p
            base = ((j - o) * 2 + key_plane) * T
            seen = (key_rows >= start_lane - base) & (key_rows <= pos_lane - base)
            bias[pl.ds((rel * SEEN + o) * T, T), :] = jnp.where(seen, 0.0, NEG_FILL)

    loads[0].wait()
    loads[1].wait()
    for h in range(HQ):
        cols = pl.ds(h * HD, HD)
        q_st[pl.ds(h * T, T), :] = q_in[:, cols]
        o_st[pl.ds(h * T, T), :] = (adv_row * og_in[:, cols].astype(jnp.float32)).astype(jnp.bfloat16)

    kf = []
    for i, half in enumerate(halves):
        kz[i].wait_recv()
        cps = [remote(kvb.at[SEEN, :, half], kvb.at[SEEN + o, :, half], kf_s.at[i], kf_r.at[i], plane(o)) for o in range(1, SEEN)]
        kf.append(whole(kvb.at[pl.ds(0, SEEN - 1), :, half], kf_s.at[i], kf_r.at[i]))
        start(cps, kf[i])
    for (axis, offset, flip), cp in x_copies.items():
        if offset != 2:
            cp.start()

    half_rows = SEEN * T

    def scores_of(rel):
        at = pl.ds(rel * half_rows, half_rows)
        keys = kvb[pl.ds(rel * SEEN, SEEN), :, :HD].reshape(half_rows, HD)
        values = kvb[pl.ds(rel * SEEN, SEEN), :, HD:].reshape(half_rows, HD)
        for h in range(HQ):
            heads = pl.ds(h * T, T)
            score[at, heads] = dot_nt(keys, q_st[heads, :]) * SCALE + bias[at, :]
            grad_prob[at, heads] = dot_nt(values, o_st[heads, :])

    loads[2].wait()
    kp_whole.wait_recv()
    scores_of(0)
    for group in kf:
        group.wait_recv()
    scores_of(1)
    for h in range(HQ):
        heads = pl.ds(h * T, T)
        scores = score[:, heads]
        weights = jnp.exp(scores - jnp.max(scores, axis=0, keepdims=True))
        probs = weights * (1.0 / jnp.sum(weights, axis=0, keepdims=True))
        row_dot = jnp.sum(probs * grad_prob[:, heads], axis=0, keepdims=True)
        ds_st[:, heads] = (probs * (grad_prob[:, heads] - row_dot)).astype(jnp.bfloat16)
        p_st[:, heads] = probs.astype(jnp.bfloat16)

    def term(rel, half):
        at = pl.ds(rel * half_rows, half_rows)
        if half == VALUE:
            return dot_nn(p_st[at, :], o_st[...])
        return dot_nn(ds_st[at, :], q_st[...]) * SCALE

    sent = {}
    for rel in (1, 0):
        for half in (VALUE, KEY):
            terms = term(rel, half)
            own_far[half, rel] = terms[:T]
            part[half, pl.ds(rel * 4, 4)] = terms[T:].astype(jnp.bfloat16).reshape(SEEN - 1, T, HD)
            at = pl.ds(rel * 4, 4)
            send, recv = d_s.at[half, rel], d_r.at[half, rel]
            cps = [remote(part.at[half, rel * 4 + o - 1], got.at[half, rel * 4 + o - 1], send, recv, plane(16 - o)) for o in range(1, SEEN)]
            sent[rel, half] = whole(got.at[half, at], send, recv)
            start(cps, sent[rel, half])

    def terms_sum(rel, half):
        sent[rel, half].wait_recv()
        total = own_far[half, rel]
        for o in range(SEEN - 1):
            total = total + got[half, rel * 4 + o].astype(jnp.float32)
        return total

    dz = []
    for half in (VALUE, KEY):
        far_sum[half] = terms_sum(1, half).astype(jnp.bfloat16)
        dz.append(remote(far_sum.at[half], far_got.at[half], dz_s.at[half], dz_r.at[half], partner))
        start([dz[half]], dz[half])
    for (axis, offset, flip), cp in x_copies.items():
        if offset == 2:
            cp.start()
    x_whole = [whole(x_all.at[axis, :, :, pl.ds(0, 7 * T)], x_s.at[axis], x_r.at[axis]) for axis in range(2)]
    sends.extend(x_whole)
    plan_row = plan[pl.ds(c, 1), :]
    out_row = lax.broadcasted_iota(jnp.int32, (4 * T, 32), 0)
    span_no = lax.broadcasted_iota(jnp.int32, (4 * T, 32), 1)
    block = jnp.sum(jnp.where(out_row // 16 == span_no, jnp.broadcast_to(plan_row, (4 * T, 32)), 0), axis=1, keepdims=True)
    row_no = lax.broadcasted_iota(jnp.int32, (4 * T, 1), 0)
    source = (row_no // 4 % 4) * T + block * 4 + row_no % 4
    for h in range(HQ):
        col_no = lax.broadcasted_iota(jnp.int32, (4 * T, T), 1) + h * T
        onehot[:, pl.ds(h * T, T)] = jnp.where(col_no == source, 1.0, 0.0).astype(jnp.bfloat16)


    for s in range(2 * SEEN):
        k_t[:, pl.ds(s * T, T)] = kvb[s, :, :HD].T
    q_grad_t = (dot_nn(k_t[...], ds_st[...]) * SCALE).astype(jnp.bfloat16)
    q_send[...] = dot_nt(onehot[...], q_grad_t).astype(jnp.bfloat16).reshape(32, 16, HD)
    q_recv[c] = q_send[c]

    def q_copy(o):
        there = lax.rem(c + o, 32)
        return remote(q_send.at[there], q_recv.at[c], qa_s, qa_r, (d, there))

    q_whole = whole(q_recv.at[pl.ds(0, 31)], qa_s, qa_r)

    start_all(q_copy, 1, 32)
    sends.append(q_whole)

    near = [terms_sum(0, half) for half in (VALUE, KEY)]

    g_copies = {}
    for half in (VALUE, KEY):
        dz[half].wait_recv()
        kvg = (near[half] + far_got[half].astype(jnp.float32)).astype(jnp.bfloat16)
        kvg_out[:, COLUMNS[half]] = kvg
        for axis in range(2):
            g_all[half, axis, own_slot[axis]] = kvg
        for axis in range(2):
            slot = g_all.at[half, axis, own_slot[axis]]
            send, recv = g_s.at[half, axis], g_r.at[half, axis]
            g_copies[half, axis] = whole(g_all.at[half, axis, pl.ds(0, 7)], send, recv)
            start([remote(slot, slot, send, recv, line(axis, offset, flip)) for offset, flip in OTHERS], g_copies[half, axis])

    for axis in range(2):
        x_whole[axis].wait_recv()
        x_own[axis].wait()

    w_copies = {}
    for half in (VALUE, KEY):
        for axis in range(2):
            g_copies[half, axis].wait_recv()
            terms = dot_nn(x_all[axis].reshape(4 * T, 8 * T), g_all[half, axis].reshape(8 * T, HD)).reshape(4, T, HD)
            w_acc[half, axis] = terms
            w_send[half, axis] = terms.astype(jnp.bfloat16)
            send, recv = w_s.at[half, axis], w_r.at[half, axis]
            cps = []
            for offset in (2, 1, 3):
                there = lax.rem(own_pos[1 - axis] + offset, 4)
                cps.append(remote(w_send.at[half, axis, there], w_got.at[half, axis * 3 + offset - 1], send, recv, line(1 - axis, offset, 0)))
            w_copies[half, axis] = whole(w_got.at[half, pl.ds(axis * 3, 3)], send, recv)
            start(cps, w_copies[half, axis])

    z_copies = []
    for half in (VALUE, KEY):
        for axis in range(2):
            w_copies[half, axis].wait_recv()
            total = w_acc[half, axis, own_pos[1 - axis]]
            for offset in range(1, 4):
                total = total + w_got[half, axis * 3 + offset - 1].astype(jnp.float32)
            w_z[half, pl.ds(axis * 8, 8)] = total.astype(jnp.bfloat16).reshape(8, 16, HD)
        w_z_got[half, z] = w_z[half, z]

        def z_copy(o, half=half):
            return remote(w_z.at[half, lax.rem(z + o, 16)], w_z_got.at[half, z], z_s.at[half], z_r.at[half], along_z(o))

        start_all(z_copy, 1, 16)
        z_copies.append(whole(w_z_got.at[half, pl.ds(0, 15)], z_s.at[half], z_r.at[half]))

    q_whole.wait_recv()
    arrived = q_recv[...].reshape(4 * T, HD)
    tok = lax.broadcasted_iota(jnp.int32, (T, 4 * T), 0)
    place = lax.broadcasted_iota(jnp.int32, (T, 4 * T), 1)
    for h in range(HQ):
        pick = jnp.where(place == tok // 4 * 16 + h * 4 + tok % 4, 1.0, 0.0).astype(jnp.bfloat16)
        qg_out[:, pl.ds(h * HD, HD)] = dot_nn(pick, arrived).astype(jnp.bfloat16)

    drain(sends)
    for half in (VALUE, KEY):
        z_copies[half].wait_recv()
        total = jnp.sum(w_z_got[half].astype(jnp.float32), axis=0)
        wg_out[:, COLUMNS[half]] = (total * (1.0 / 256.0)).astype(jnp.bfloat16)
    drain(z_copies)


def local(normed, query, key_value, output_grad, lengths, advantage, span_plan):
    bf16, f32 = jnp.bfloat16, jnp.float32
    n_keys = 2 * SEEN * T
    dma = pltpu.SemaphoreType.DMA
    vmem = pl.BlockSpec(memory_space=pltpu.VMEM)
    return pl.pallas_call(
        kernel,
        out_shape=(
            jax.ShapeDtypeStruct((T, HQ * HD), bf16),
            jax.ShapeDtypeStruct((T, 2 * HD), bf16),
            jax.ShapeDtypeStruct((16, 2 * HD), bf16),
        ),
        in_specs=[pl.BlockSpec(memory_space=pltpu.HBM)] * 7,
        out_specs=(vmem, vmem, vmem),
        scratch_shapes=[
            pltpu.SMEM((1, 16), jnp.int32),
            pltpu.SMEM((1, 16), f32),
            pltpu.VMEM((32, 32), jnp.int32),
            pltpu.VMEM((T, HQ * HD), bf16),
            pltpu.VMEM((T, HQ * HD), bf16),
            pltpu.VMEM((HQ * T, HD), bf16),
            pltpu.VMEM((HQ * T, HD), bf16),
            pltpu.VMEM((2 * SEEN, T, 2 * HD), bf16),
            pltpu.VMEM((HD, n_keys), bf16),
            pltpu.VMEM((n_keys, T), f32),
            pltpu.VMEM((n_keys, HQ * T), f32),
            pltpu.VMEM((n_keys, HQ * T), f32),
            pltpu.VMEM((n_keys, HQ * T), bf16),
            pltpu.VMEM((n_keys, HQ * T), bf16),
            pltpu.VMEM((HQ * T, HQ * T), bf16),
            pltpu.VMEM((2, 8, T, HD), bf16),
            pltpu.VMEM((2, 8, T, HD), bf16),
            pltpu.VMEM((2, 2, T, HD), f32),
            pltpu.VMEM((2, T, HD), bf16),
            pltpu.VMEM((2, T, HD), bf16),
            pltpu.VMEM((32, 16, HD), bf16),
            pltpu.VMEM((32, 16, HD), bf16),
            pltpu.VMEM((T, 16 * FEAT), bf16),
            pltpu.VMEM((2, 2, 4, 4, T, T), bf16),
            pltpu.VMEM((2, 4, T, 8 * T), bf16),
            pltpu.VMEM((2, 2, 8, T, HD), bf16),
            pltpu.VMEM((2, 2, 4, T, HD), f32),
            pltpu.VMEM((2, 2, 4, T, HD), bf16),
            pltpu.VMEM((2, 6, T, HD), bf16),
            pltpu.VMEM((2, 16, 16, HD), bf16),
            pltpu.VMEM((2, 16, 16, HD), bf16),
            dma((9,)), dma((2,)), dma((2,)), dma, dma, dma((2,)), dma((2,)),
            dma((2,)), dma((2,)), dma((2, 2)), dma((2, 2)), dma((2,)), dma((2,)), dma, dma,
            dma((2, 2)), dma((2, 2)), dma((2, 2)), dma((2, 2)), dma((2,)), dma((2,)),
        ],
        compiler_params=pltpu.CompilerParams(collective_id=0, has_side_effects=True, vmem_limit_bytes=48 * 2**20),
        name="backward",
    )(*[pltpu.with_memory_space_constraint(a, pltpu.HBM) for a in (normed, query, key_value, output_grad, lengths, advantage, span_plan)])


def solution(mesh):
    return jax.shard_map(
        local,
        mesh=mesh,
        in_specs=(
            P(("dp", "ctx"), None),
            P(("dp", "ctx"), None),
            P(("dp", "ctx"), None),
            P(("dp", "ctx"), None),
            P("dp", None),
            P("dp", None),
            P("dp", None, None),
        ),
        out_specs=(P(("dp", "ctx"), None), P(("dp", "ctx"), None), P(("ctx", "dp"), None)),
        check_vma=False,
    )
```

```python
import jax
import jax.numpy as jnp
from jax import lax
from jax.experimental import pallas as pl
from jax.experimental.pallas import tpu as pltpu
from jax.sharding import PartitionSpec as P

NEG_FILL = -1e30
MESH = pl.DeviceIdType.MESH
T = 128
HQ = 4
HD = 128
SEEN = 5
FEAT = 512
SCALE = HD**-0.5
OTHERS = [(2, 0), (2, 1), (1, 0), (1, 1), (3, 0), (3, 1), (0, 1)]
VALUE, KEY = 0, 1
COLUMNS = [pl.ds(HD, HD), pl.ds(0, HD)]


def dot_nt(a, b):
    return lax.dot_general(a, b, (((1,), (1,)), ((), ())), preferred_element_type=jnp.float32)


def dot_nn(a, b):
    return lax.dot_general(a, b, (((1,), (0,)), ((), ())), preferred_element_type=jnp.float32)


def kernel(normed, query, kv, og, lengths_in, advantage_in, plan_in, qg_out, kvg_out, wg_out,
           lengths, advantage, plan, q_in, og_in, q_st, o_st, kvb, k_t, bias, score, grad_prob, p_st, ds_st, onehot, part, got, own_far, far_sum, far_got,
           q_send, q_recv, x_in, x_t, x_all, g_all, w_acc, w_send, w_got, w_z, w_z_got,
           loc_sem, kz_s, kz_r, kp_s, kp_r, kf_s, kf_r, x_s, x_r, d_s, d_r, dz_s, dz_r, qa_s, qa_r, g_s, g_r, w_s, w_r, z_s, z_r):
    d = lax.axis_index("dp")
    c = lax.axis_index("ctx")
    j, p = c // 2, c % 2
    z_lo, core = d // 2, d % 2
    z = p * 8 + z_lo
    y, x = j // 4, lax.rem(j, 4)
    own_slot = (x * 2 + core, y * 2 + core)
    own_pos = (x, y)

    def plane(offset):
        return (d, lax.rem(j + offset, 16) * 2 + p)

    partner = (d, j * 2 + (1 - p))

    def line(axis, offset, flip):
        to_core = core if flip == 0 else 1 - core
        to_x = lax.rem(x + offset, 4) if axis == 0 else x
        to_y = lax.rem(y + offset, 4) if axis == 1 else y
        return (z_lo * 2 + to_core, (to_y * 4 + to_x) * 2 + p)

    def along_z(offset):
        there = lax.rem(z + offset, 16)
        return (lax.rem(there, 8) * 2 + core, j * 2 + there // 8)

    def remote(src, dst, send, recv, where):
        return pltpu.make_async_remote_copy(src_ref=src, dst_ref=dst, send_sem=send, recv_sem=recv,
                                            device_id=where, device_id_type=MESH)

    sends = []

    def whole(ref, send, recv):
        return remote(ref, ref, send, recv, partner)

    def start(cps, group):
        for cp in cps:
            cp.start()
        sends.append(group)

    def start_all(make, low, high):
        for o in range(low, high):
            make(o).start()

    def drain(items):
        for cp in items:
            cp.wait_send()

    barrier = pltpu.get_barrier_semaphore()

    def greet(where):
        pl.semaphore_signal(barrier, inc=1, device_id=where, device_id_type=MESH)

    for o in range(16):
        greet((d, lax.rem(j + o, 16) * 2 + (1 - p)))
    for o in range(1, 16):
        if o != 8:
            greet(along_z(o))
    for o in range(1, 16):
        greet(plane(o))
    for axis, offset in [(0, 0), (0, 1), (0, 2), (0, 3), (1, 1), (1, 2), (1, 3)]:
        pl.semaphore_signal(barrier, inc=1, device_id=line(axis, offset, 1), device_id_type=MESH)
    loads = [
        pltpu.make_async_copy(query, q_in, loc_sem.at[0]),
        pltpu.make_async_copy(og, og_in, loc_sem.at[1]),
        pltpu.make_async_copy(kv, kvb.at[0], loc_sem.at[2]),
        pltpu.make_async_copy(normed, x_in, loc_sem.at[3]),
        pltpu.make_async_copy(lengths_in, lengths, loc_sem.at[4]),
        pltpu.make_async_copy(advantage_in, advantage, loc_sem.at[5]),
        pltpu.make_async_copy(plan_in.at[0], plan, loc_sem.at[6]),
    ]
    for cp in loads:
        cp.start()

    pl.semaphore_wait(barrier, 52)

    halves = [pl.ds(0, HD), pl.ds(HD, HD)]
    kz = [remote(kv.at[:, half], kvb.at[SEEN, :, half], kz_s.at[i], kz_r.at[i], partner) for i, half in enumerate(halves)]
    for cp in kz:
        start([cp], cp)
    kp = [remote(kv, kvb.at[o], kp_s, kp_r, plane(o)) for o in range(1, SEEN)]
    kp_whole = whole(kvb.at[pl.ds(0, SEEN - 1)], kp_s, kp_r)
    start(kp, kp_whole)

    loads[3].wait()

    def turn(at, carry):
        for q in range(4):
            block = x_in[:, pl.ds(pl.multiple_of(at * FEAT + q * T, T), T)].T
            for low in range(4):
                for k in range(2):
                    x_t[q // 2, k, at // 4, lax.rem(at, 4), pl.ds(((q % 2) * 4 + low) * 16, 16), :] = (
                        block[(low * 2 + k) * 16 : (low * 2 + k + 1) * 16])
        return carry

    lax.fori_loop(0, 16, turn, 0)

    def x_source(axis, offset, flip):
        to_core = core if flip == 0 else 1 - core
        if axis == 0:
            return x_t.at[0, to_core, :, lax.rem(x + offset, 4)]
        return x_t.at[1, to_core, lax.rem(y + offset, 4)]

    def x_place(axis):
        return x_all.at[axis, :, :, pl.ds(pl.multiple_of(own_slot[axis] * T, T), T)]

    x_copies = {}
    for axis in range(2):
        for offset, flip in OTHERS:
            x_copies[axis, offset, flip] = remote(x_source(axis, offset, flip), x_place(axis), x_s.at[axis], x_r.at[axis], line(axis, offset, flip))
    x_own = [pltpu.make_async_copy(x_source(axis, 0, 0), x_place(axis), loc_sem.at[7 + axis]) for axis in range(2)]
    for cp in x_own:
        cp.start()

    for cp in loads[4:]:
        cp.wait()
    lanes = lax.broadcasted_iota(jnp.int32, (1, T), 1)
    rows = lax.broadcasted_iota(jnp.int32, (T, HD), 0)
    pos_lane = c * T + lanes
    pos_row = c * T + rows
    start_lane = jnp.zeros((1, T), jnp.int32)
    adv_row = jnp.zeros((T, HD), jnp.float32)
    end = jnp.int32(0)
    for i in range(16):
        begin = end
        end = end + lengths[0, i]
        start_lane = jnp.where(pos_lane >= begin, begin, start_lane)
        adv_row = jnp.where(pos_row >= begin, advantage[0, i], adv_row)
    key_rows = lax.broadcasted_iota(jnp.int32, (T, T), 0)
    for rel in range(2):
        for o in range(SEEN):
            key_plane = p if rel == 0 else 1 - p
            base = ((j - o) * 2 + key_plane) * T
            seen = (key_rows >= start_lane - base) & (key_rows <= pos_lane - base)
            bias[pl.ds((rel * SEEN + o) * T, T), :] = jnp.where(seen, 0.0, NEG_FILL)

    loads[0].wait()
    loads[1].wait()
    for h in range(HQ):
        cols = pl.ds(h * HD, HD)
        q_st[pl.ds(h * T, T), :] = q_in[:, cols]
        o_st[pl.ds(h * T, T), :] = (adv_row * og_in[:, cols].astype(jnp.float32)).astype(jnp.bfloat16)

    kf = []
    for i, half in enumerate(halves):
        kz[i].wait_recv()
        cps = [remote(kvb.at[SEEN, :, half], kvb.at[SEEN + o, :, half], kf_s.at[i], kf_r.at[i], plane(o)) for o in range(1, SEEN)]
        kf.append(whole(kvb.at[pl.ds(0, SEEN - 1), :, half], kf_s.at[i], kf_r.at[i]))
        start(cps, kf[i])
    for (axis, offset, flip), cp in x_copies.items():
        if offset != 2:
            cp.start()

    half_rows = SEEN * T

    def scores_of(rel):
        at = pl.ds(rel * half_rows, half_rows)
        keys = kvb[pl.ds(rel * SEEN, SEEN), :, :HD].reshape(half_rows, HD)
        values = kvb[pl.ds(rel * SEEN, SEEN), :, HD:].reshape(half_rows, HD)
        for h in range(HQ):
            heads = pl.ds(h * T, T)
            score[at, heads] = dot_nt(keys, q_st[heads, :]) * SCALE + bias[at, :]
            grad_prob[at, heads] = dot_nt(values, o_st[heads, :])

    loads[2].wait()
    kp_whole.wait_recv()
    scores_of(0)
    for group in kf:
        group.wait_recv()
    scores_of(1)
    for h in range(HQ):
        heads = pl.ds(h * T, T)
        scores = score[:, heads]
        weights = jnp.exp(scores - jnp.max(scores, axis=0, keepdims=True))
        probs = weights * (1.0 / jnp.sum(weights, axis=0, keepdims=True))
        row_dot = jnp.sum(probs * grad_prob[:, heads], axis=0, keepdims=True)
        ds_st[:, heads] = (probs * (grad_prob[:, heads] - row_dot)).astype(jnp.bfloat16)
        p_st[:, heads] = probs.astype(jnp.bfloat16)

    def term(rel, half):
        at = pl.ds(rel * half_rows, half_rows)
        if half == VALUE:
            return dot_nn(p_st[at, :], o_st[...])
        return dot_nn(ds_st[at, :], q_st[...]) * SCALE

    sent = {}
    for rel in (1, 0):
        for half in (VALUE, KEY):
            terms = term(rel, half)
            own_far[half, rel] = terms[:T]
            part[half, pl.ds(rel * 4, 4)] = terms[T:].astype(jnp.bfloat16).reshape(SEEN - 1, T, HD)
            at = pl.ds(rel * 4, 4)
            send, recv = d_s.at[half, rel], d_r.at[half, rel]
            cps = [remote(part.at[half, rel * 4 + o - 1], got.at[half, rel * 4 + o - 1], send, recv, plane(16 - o)) for o in range(1, SEEN)]
            sent[rel, half] = whole(got.at[half, at], send, recv)
            start(cps, sent[rel, half])

    def terms_sum(rel, half):
        sent[rel, half].wait_recv()
        total = own_far[half, rel]
        for o in range(SEEN - 1):
            total = total + got[half, rel * 4 + o].astype(jnp.float32)
        return total

    dz = []
    for half in (VALUE, KEY):
        far_sum[half] = terms_sum(1, half).astype(jnp.bfloat16)
        dz.append(remote(far_sum.at[half], far_got.at[half], dz_s.at[half], dz_r.at[half], partner))
        start([dz[half]], dz[half])
    for (axis, offset, flip), cp in x_copies.items():
        if offset == 2:
            cp.start()
    x_whole = [whole(x_all.at[axis, :, :, pl.ds(0, 7 * T)], x_s.at[axis], x_r.at[axis]) for axis in range(2)]
    sends.extend(x_whole)
    plan_row = plan[pl.ds(c, 1), :]
    out_row = lax.broadcasted_iota(jnp.int32, (4 * T, 32), 0)
    span_no = lax.broadcasted_iota(jnp.int32, (4 * T, 32), 1)
    block = jnp.sum(jnp.where(out_row // 16 == span_no, jnp.broadcast_to(plan_row, (4 * T, 32)), 0), axis=1, keepdims=True)
    row_no = lax.broadcasted_iota(jnp.int32, (4 * T, 1), 0)
    source = (row_no // 4 % 4) * T + block * 4 + row_no % 4
    for h in range(HQ):
        col_no = lax.broadcasted_iota(jnp.int32, (4 * T, T), 1) + h * T
        onehot[:, pl.ds(h * T, T)] = jnp.where(col_no == source, 1.0, 0.0).astype(jnp.bfloat16)


    for s in range(2 * SEEN):
        k_t[:, pl.ds(s * T, T)] = kvb[s, :, :HD].T
    q_grad_t = (dot_nn(k_t[...], ds_st[...]) * SCALE).astype(jnp.bfloat16)
    q_send[...] = dot_nt(onehot[...], q_grad_t).astype(jnp.bfloat16).reshape(32, 16, HD)
    q_recv[c] = q_send[c]

    def q_copy(o):
        there = lax.rem(c + o, 32)
        return remote(q_send.at[there], q_recv.at[c], qa_s, qa_r, (d, there))

    q_whole = whole(q_recv.at[pl.ds(0, 31)], qa_s, qa_r)

    start_all(q_copy, 1, 32)
    sends.append(q_whole)

    near = [terms_sum(0, half) for half in (VALUE, KEY)]

    g_copies = {}
    for half in (VALUE, KEY):
        dz[half].wait_recv()
        kvg = (near[half] + far_got[half].astype(jnp.float32)).astype(jnp.bfloat16)
        kvg_out[:, COLUMNS[half]] = kvg
        for axis in range(2):
            g_all[half, axis, own_slot[axis]] = kvg
        for axis in range(2):
            slot = g_all.at[half, axis, own_slot[axis]]
            send, recv = g_s.at[half, axis], g_r.at[half, axis]
            g_copies[half, axis] = whole(g_all.at[half, axis, pl.ds(0, 7)], send, recv)
            start([remote(slot, slot, send, recv, line(axis, offset, flip)) for offset, flip in OTHERS], g_copies[half, axis])

    for axis in range(2):
        x_whole[axis].wait_recv()
        x_own[axis].wait()

    w_copies = {}
    for half in (VALUE, KEY):
        for axis in range(2):
            g_copies[half, axis].wait_recv()
            terms = dot_nn(x_all[axis].reshape(4 * T, 8 * T), g_all[half, axis].reshape(8 * T, HD)).reshape(4, T, HD)
            w_acc[half, axis] = terms
            w_send[half, axis] = terms.astype(jnp.bfloat16)
            send, recv = w_s.at[half, axis], w_r.at[half, axis]
            cps = []
            for offset in (2, 1, 3):
                there = lax.rem(own_pos[1 - axis] + offset, 4)
                cps.append(remote(w_send.at[half, axis, there], w_got.at[half, axis * 3 + offset - 1], send, recv, line(1 - axis, offset, 0)))
            w_copies[half, axis] = whole(w_got.at[half, pl.ds(axis * 3, 3)], send, recv)
            start(cps, w_copies[half, axis])

    z_copies = []
    for half in (VALUE, KEY):
        for axis in range(2):
            w_copies[half, axis].wait_recv()
            total = w_acc[half, axis, own_pos[1 - axis]]
            for offset in range(1, 4):
                total = total + w_got[half, axis * 3 + offset - 1].astype(jnp.float32)
            w_z[half, pl.ds(axis * 8, 8)] = total.astype(jnp.bfloat16).reshape(8, 16, HD)
        w_z_got[half, z] = w_z[half, z]

        def z_copy(o, half=half):
            return remote(w_z.at[half, lax.rem(z + o, 16)], w_z_got.at[half, z], z_s.at[half], z_r.at[half], along_z(o))

        for o in sorted(range(1, 16), key=lambda o: -min(o, 16 - o)):
            z_copy(o).start()
        z_copies.append(whole(w_z_got.at[half, pl.ds(0, 15)], z_s.at[half], z_r.at[half]))

    q_whole.wait_recv()
    arrived = q_recv[...].reshape(4 * T, HD)
    tok = lax.broadcasted_iota(jnp.int32, (T, 4 * T), 0)
    place = lax.broadcasted_iota(jnp.int32, (T, 4 * T), 1)
    for h in range(HQ):
        pick = jnp.where(place == tok // 4 * 16 + h * 4 + tok % 4, 1.0, 0.0).astype(jnp.bfloat16)
        qg_out[:, pl.ds(h * HD, HD)] = dot_nn(pick, arrived).astype(jnp.bfloat16)

    drain(sends)
    for half in (VALUE, KEY):
        z_copies[half].wait_recv()
        total = jnp.sum(w_z_got[half].astype(jnp.float32), axis=0)
        wg_out[:, COLUMNS[half]] = (total * (1.0 / 256.0)).astype(jnp.bfloat16)
    drain(z_copies)


def local(normed, query, key_value, output_grad, lengths, advantage, span_plan):
    bf16, f32 = jnp.bfloat16, jnp.float32
    n_keys = 2 * SEEN * T
    dma = pltpu.SemaphoreType.DMA
    vmem = pl.BlockSpec(memory_space=pltpu.VMEM)
    return pl.pallas_call(
        kernel,
        out_shape=(
            jax.ShapeDtypeStruct((T, HQ * HD), bf16),
            jax.ShapeDtypeStruct((T, 2 * HD), bf16),
            jax.ShapeDtypeStruct((16, 2 * HD), bf16),
        ),
        in_specs=[pl.BlockSpec(memory_space=pltpu.HBM)] * 7,
        out_specs=(vmem, vmem, vmem),
        scratch_shapes=[
            pltpu.SMEM((1, 16), jnp.int32),
            pltpu.SMEM((1, 16), f32),
            pltpu.VMEM((32, 32), jnp.int32),
            pltpu.VMEM((T, HQ * HD), bf16),
            pltpu.VMEM((T, HQ * HD), bf16),
            pltpu.VMEM((HQ * T, HD), bf16),
            pltpu.VMEM((HQ * T, HD), bf16),
            pltpu.VMEM((2 * SEEN, T, 2 * HD), bf16),
            pltpu.VMEM((HD, n_keys), bf16),
            pltpu.VMEM((n_keys, T), f32),
            pltpu.VMEM((n_keys, HQ * T), f32),
            pltpu.VMEM((n_keys, HQ * T), f32),
            pltpu.VMEM((n_keys, HQ * T), bf16),
            pltpu.VMEM((n_keys, HQ * T), bf16),
            pltpu.VMEM((HQ * T, HQ * T), bf16),
            pltpu.VMEM((2, 8, T, HD), bf16),
            pltpu.VMEM((2, 8, T, HD), bf16),
            pltpu.VMEM((2, 2, T, HD), f32),
            pltpu.VMEM((2, T, HD), bf16),
            pltpu.VMEM((2, T, HD), bf16),
            pltpu.VMEM((32, 16, HD), bf16),
            pltpu.VMEM((32, 16, HD), bf16),
            pltpu.VMEM((T, 16 * FEAT), bf16),
            pltpu.VMEM((2, 2, 4, 4, T, T), bf16),
            pltpu.VMEM((2, 4, T, 8 * T), bf16),
            pltpu.VMEM((2, 2, 8, T, HD), bf16),
            pltpu.VMEM((2, 2, 4, T, HD), f32),
            pltpu.VMEM((2, 2, 4, T, HD), bf16),
            pltpu.VMEM((2, 6, T, HD), bf16),
            pltpu.VMEM((2, 16, 16, HD), bf16),
            pltpu.VMEM((2, 16, 16, HD), bf16),
            dma((9,)), dma((2,)), dma((2,)), dma, dma, dma((2,)), dma((2,)),
            dma((2,)), dma((2,)), dma((2, 2)), dma((2, 2)), dma((2,)), dma((2,)), dma, dma,
            dma((2, 2)), dma((2, 2)), dma((2, 2)), dma((2, 2)), dma((2,)), dma((2,)),
        ],
        compiler_params=pltpu.CompilerParams(collective_id=0, has_side_effects=True, vmem_limit_bytes=48 * 2**20),
        name="backward",
    )(*[pltpu.with_memory_space_constraint(a, pltpu.HBM) for a in (normed, query, key_value, output_grad, lengths, advantage, span_plan)])


def solution(mesh):
    return jax.shard_map(
        local,
        mesh=mesh,
        in_specs=(
            P(("dp", "ctx"), None),
            P(("dp", "ctx"), None),
            P(("dp", "ctx"), None),
            P(("dp", "ctx"), None),
            P("dp", None),
            P("dp", None),
            P("dp", None, None),
        ),
        out_specs=(P(("dp", "ctx"), None), P(("dp", "ctx"), None), P(("ctx", "dp"), None)),
        check_vma=False,
    )
```
